256 devices in a mesh: dp: 16 (over y, x), expert: 16 (over z, core).
Axes of the slice: x: 4, y: 4, z: 8, core: 2. Of those that a mesh axis runs over, the one named last changes fastest.
Arguments:
- tokens: bfloat16 [8192, 2048], P('dp'), may hold values from -6 to 6
- routes: int32 [8192, 6], P('dp'), may hold values from 0 to 63, all different within a row; in each aligned block of 512 rows (0 to 511, 512 to 1023, ...) at most 72 rows name the same one
- route_weight: float32 [8192, 6], P('dp'), may hold values from 0.05 to 0.5
- w_gate: bfloat16 [256, 352, 2048], P(('dp', 'expert')), may hold values from -0.125 to 0.125
- w_up: bfloat16 [256, 352, 2048], P(('dp', 'expert')), may hold values from -0.125 to 0.125
- w_down: bfloat16 [256, 352, 2048], P(('dp', 'expert')), may hold values from -0.15625 to 0.15625
- grad_out: bfloat16 [8192, 2048], P(('dp', 'expert')), may hold values from -6 to 6
Outputs:
- mixed: bfloat16 [8192, 2048], P(('dp', 'expert'))
- grad_tokens: bfloat16 [8192, 2048], P(('dp', 'expert'))
- grad_route_weight: float32 [8192, 6], P(('dp', 'expert'))
- grad_gate: bfloat16 [256, 352, 2048], P(('dp', 'expert'))
- grad_up: bfloat16 [256, 352, 2048], P(('dp', 'expert'))
- grad_down: bfloat16 [256, 352, 2048], P(('dp', 'expert'))
The draws below stay inside these ranges and needn't reach their ends.
Inputs may be any that keep to these rules, and one draw needn't show every extreme that they name: `routes`: each row names 6 different experts. Within the 512 rows of one index of dp no expert is named by more than 72 rows.
All inputs are finite; a program needn't handle non-finite values.
Results may differ from the reference program's by a relative error of at most 0.023.
Values may be sent and summed in bfloat16 or wider, within the bound.
A program may use at most 192 MiB of HBM per device.

```python
import math
import jax
import jax.numpy as jnp
import numpy as np
from jax import lax

D = 2048
FF = 1408
TOP = 6
SHARDS = 4
TOK_DP = 512
EXPERTS = 64
FF_DEV = 352
CAP = 72
TOKENS = 8192
N_DP = 16


def block_scale(stream_key, extent, split, low, largest):
    gain = 1.0
    for position, shards_of in split:
        steps = jax.random.uniform(jax.random.fold_in(jax.random.fold_in(stream_key, 6), position), (shards_of,), jnp.float32, low / len(split), largest / len(split))
        gain = gain * jnp.repeat(jnp.exp(steps), extent[position] // shards_of).reshape((-1,) + (1,) * (len(extent) - 1 - position))
    return gain


def shared_out(stream_key, own, number, rows, amount, top, bound, slope):
    sequence = jax.random.permutation(stream_key, amount)
    packed, common = load_shares(amount, rows * top, bound, slope, True), load_shares(amount, rows * top, bound, slope, False)
    places = jnp.arange(amount)

    def named(lengths, rotation):
        used = int((lengths > 0).sum())
        fixed = max(1, used // 4)
        passed = fixed + (places - fixed + rotation * (used - fixed)) % max(1, amount - fixed)
        return jnp.zeros((amount,), jnp.int32).at[sequence[jnp.where(places < fixed, places, passed)]].set(jnp.asarray(lengths, jnp.int32))

    lengths = jnp.where(number % 4 == 0, named(packed, number // 4), named(common, number - number // 4 - 1))
    mixed = jax.random.permutation(jax.random.fold_in(own, 3), amount)
    giver, taker = mixed[0:amount // 2 * 2:2], mixed[1:amount // 2 * 2:2]
    slack = jnp.minimum(lengths[giver] - 1, bound - lengths[taker]) // 2
    slack = jnp.where((giver == sequence[0]) | (taker == sequence[0]) | (lengths[taker] == 0), 0, jnp.maximum(slack, 0))
    passed = jax.random.randint(jax.random.fold_in(own, 4), (amount // 2,), 0, 1 << 20) % (slack + 1)
    lengths = lengths.at[giver].add(-passed).at[taker].add(passed)
    items = jnp.searchsorted(jnp.cumsum(lengths), jnp.arange(rows * top), side="right").astype(jnp.int32)
    listing = items.reshape(top, rows).T
    listing = listing[jax.random.permutation(jax.random.fold_in(own, 1), rows)]
    rotation = jax.random.randint(jax.random.fold_in(own, 2), (rows, 1), 0, top)
    return jnp.take_along_axis(listing, (jnp.arange(top)[None, :] + rotation) % top, axis=1)


def load_shares(count, total, reach, lean, full):
    weights = [(1 << 20) // math.isqrt(grade ** lean) + 1 for grade in range(1, count + 1)]
    largest = reach if full else min(reach, max(-(-total // count), total * weights[0] // sum(weights)))
    least = 1 if total - largest >= count - 1 else 0
    given, surplus = [largest] + [least] * (count - 1), total - largest - least * (count - 1)
    while surplus > 0:
        movable = [i for i in range(1, count) if given[i] < largest] or [i for i in range(1, count) if given[i] < reach]
        pool, left = sum([weights[i] for i in movable]), surplus
        for i in movable:
            more = min(reach - given[i], max(1, left * weights[i] // pool), surplus)
            given[i] = given[i] + more
            surplus = surplus - more
    return np.array(given)


def normal_values(stream_key, dims, scale, limit, split=(), held_as=jnp.bfloat16):
    drawn = jax.random.normal(stream_key, dims, jnp.float32) * scale
    if len(split) > 0:
        drawn = block_scale(stream_key, dims, split, -0.22, 0.18) * drawn
    return jnp.clip(drawn, min=-limit, max=limit).astype(held_as)


def setup_inputs(seed: int = 0) -> dict:
    keys = jax.random.split(jax.random.key(seed), 8)
    tokens = normal_values(keys[0], (TOKENS, D), 1.0, 6.0, ((0, 16),))
    routes_keys = jax.random.split(jax.random.fold_in(keys[1], 1), TOKENS // TOK_DP)
    routes_turns = jax.random.permutation(jax.random.fold_in(keys[1], 3), TOKENS // TOK_DP)
    routes = jax.vmap(lambda own, number: shared_out(jax.random.fold_in(keys[1], 2), own, number, TOK_DP, EXPERTS, TOP, CAP, 2))(routes_keys, routes_turns).reshape((TOKENS, TOP))
    route_weight = jnp.clip(jnp.exp(math.log(0.5) - 2.3025851 * jax.random.uniform(keys[2], (TOKENS, TOP), jnp.float32) ** block_scale(keys[2], (TOKENS, TOP), ((0, 16),), -0.2, 0.2)), 0.05, 0.5)
    w_gate = normal_values(keys[3], (EXPERTS * SHARDS, FF_DEV, D), D ** -0.5, 0.125, ((0, 256),))
    w_up = normal_values(keys[4], (EXPERTS * SHARDS, FF_DEV, D), D ** -0.5, 0.125, ((0, 256),))
    w_down = normal_values(keys[5], (EXPERTS * SHARDS, FF_DEV, D), FF ** -0.5, 0.15625, ((0, 256),))
    grad_out = normal_values(keys[6], (TOKENS, D), 1.0, 6.0, ((0, 256),))
    return {"tokens": tokens, "routes": routes, "route_weight": route_weight, "w_gate": w_gate, "w_up": w_up, "w_down": w_down, "grad_out": grad_out}


def silu_parts(gate_pre):
    sigma = jax.nn.sigmoid(gate_pre)
    return gate_pre * sigma, sigma * (1.0 + gate_pre * (1.0 - sigma))


def reference(tokens, routes, route_weight, w_gate, w_up, w_down, grad_out):
    tok_count, top_count = routes.shape
    width = tokens.shape[1]
    ff_dev = w_gate.shape[1]
    expert_count = w_gate.shape[0] // SHARDS
    hidden_width = ff_dev * SHARDS
    flat_routes = routes.reshape(-1)
    route_count = flat_routes.shape[0]
    most_rows = N_DP * CAP
    weights_flat = route_weight.reshape(-1)
    gate_all = w_gate.reshape(expert_count, hidden_width, width)
    up_all = w_up.reshape(expert_count, hidden_width, width)
    down_all = w_down.reshape(expert_count, hidden_width, width)

    def expert_step(carry, inputs):
        mixed_acc, dx_acc, grad_acc = carry
        expert_id, gate_matrix, up_matrix, down_matrix = inputs
        picked = jnp.nonzero(flat_routes == expert_id, size=most_rows, fill_value=route_count)[0].astype(jnp.int32)
        is_live = picked < route_count
        safe_index = jnp.where(is_live, picked, 0).astype(jnp.int32)
        token_of = (safe_index // top_count).astype(jnp.int32)
        x_rows = jnp.where(is_live[:, None], tokens[token_of], jnp.zeros((), tokens.dtype))
        gate_pre = jnp.dot(x_rows, gate_matrix.T, preferred_element_type=jnp.float32)
        up_pre = jnp.dot(x_rows, up_matrix.T, preferred_element_type=jnp.float32)
        silu_value, silu_slope = silu_parts(gate_pre)
        hidden = (silu_value * up_pre).astype(jnp.bfloat16)
        rows = hidden.shape[0]
        down_blocks = down_matrix.reshape(SHARDS, ff_dev, width).astype(jnp.float32)
        shard_part = jnp.einsum("rsf,sfd->rsd", hidden.reshape(rows, SHARDS, ff_dev).astype(jnp.float32), down_blocks).astype(jnp.bfloat16)
        weight_rows = jnp.where(is_live, weights_flat[safe_index], jnp.zeros((), weights_flat.dtype))
        part_sum = jnp.sum(shard_part.astype(jnp.float32), axis=1)
        mixed_acc = mixed_acc.at[token_of].add(weight_rows[:, None] * part_sum)
        cot_rows = grad_out[token_of]
        route_grad = jnp.sum(cot_rows.astype(jnp.float32)[:, None, :] * shard_part.astype(jnp.float32), axis=(1, 2))
        grad_acc = grad_acc.at[safe_index].add(jnp.where(is_live, route_grad, jnp.zeros((), route_grad.dtype)))
        route_cot = (weight_rows[:, None] * cot_rows.astype(jnp.float32)).astype(jnp.bfloat16)
        d_hidden = jnp.dot(route_cot, down_matrix.T, preferred_element_type=jnp.float32)
        d_gate = (d_hidden * up_pre * silu_slope).astype(jnp.bfloat16)
        d_up = (d_hidden * silu_value).astype(jnp.bfloat16)
        grad_down = jnp.dot(hidden.T, route_cot, preferred_element_type=jnp.float32).astype(jnp.bfloat16)
        grad_gate = jnp.dot(d_gate.T, x_rows, preferred_element_type=jnp.float32).astype(jnp.bfloat16)
        grad_up = jnp.dot(d_up.T, x_rows, preferred_element_type=jnp.float32).astype(jnp.bfloat16)
        gate_blocks = gate_matrix.reshape(SHARDS, ff_dev, width).astype(jnp.float32)
        up_blocks = up_matrix.reshape(SHARDS, ff_dev, width).astype(jnp.float32)
        shard_dx = jnp.einsum("rsf,sfd->rsd", d_gate.reshape(rows, SHARDS, ff_dev).astype(jnp.float32), gate_blocks)
        shard_dx = shard_dx + jnp.einsum("rsf,sfd->rsd", d_up.reshape(rows, SHARDS, ff_dev).astype(jnp.float32), up_blocks)
        shard_dx = shard_dx.astype(jnp.bfloat16)
        dx_sum = jnp.sum(shard_dx.astype(jnp.float32), axis=1)
        dx_acc = dx_acc.at[token_of].add(jnp.where(is_live[:, None], dx_sum, jnp.zeros((), dx_sum.dtype)))
        return (mixed_acc, dx_acc, grad_acc), (grad_gate, grad_up, grad_down)

    start = (jnp.zeros((tok_count, width), jnp.float32), jnp.zeros((tok_count, width), jnp.float32), jnp.zeros((route_count,), jnp.float32))
    carry, grads = lax.scan(expert_step, start, (jnp.arange(expert_count, dtype=jnp.int32), gate_all, up_all, down_all))
    mixed_acc, dx_acc, grad_acc = carry
    grad_gate = grads[0].reshape(expert_count * SHARDS, ff_dev, width)
    grad_up = grads[1].reshape(expert_count * SHARDS, ff_dev, width)
    grad_down = grads[2].reshape(expert_count * SHARDS, ff_dev, width)
    return (mixed_acc.astype(jnp.bfloat16), dx_acc.astype(jnp.bfloat16), grad_acc.reshape(tok_count, top_count), grad_gate, grad_up, grad_down)
```

```python
import jax
import jax.numpy as jnp
from jax import lax
from jax.experimental import pallas as pl
from jax.experimental.pallas import tpu as pltpu
from jax.sharding import PartitionSpec as P

MESH = pl.DeviceIdType.MESH
F32 = jnp.float32
BF16 = jnp.bfloat16

TOK = 512
D = 2048
HALF = 1024
FF = 352
TOP = 6
CAP = 72
T8 = CAP // 8
NDP = 16
NEX = 16
BLK = TOK // NEX
ROWS = 4 * CAP
COLS = 512


def rows_of(ref_value):
    return ref_value.reshape(-1, ref_value.shape[-1])


def nt(a, b):
    return lax.dot_general(a, b, (((1,), (1,)), ((), ())), preferred_element_type=F32)


def tn(a, b):
    return lax.dot_general(a, b, (((0,), (0,)), ((), ())), preferred_element_type=F32)


def nn(a, b):
    return jnp.dot(a, b, preferred_element_type=F32)


def kernel(
    tok_hbm, routes_ref, weight_ref, wg_hbm, wu_hbm, wd_hbm, g_hbm,
    mixed_ref, dx_ref, grw_ref, gg_hbm, gu_hbm, gd_hbm,
    tok, gloc, gall, wg, wu, wd, hits, rank, wtok, sel,
    xs, xr, gs, gr, ws, wr, vs, vret,
    yo, ypo, ypi, yret, do, dpo, dpi, dret,
    gate_s, up_s, hwt, dgt, dut,
    mst, mrecv, dst_, drecv, rst, rrecv, gg, gu, gd,
    in_sem, out_sem, sgz, rgz, sx, rx, sxf, rxf, sw, rw, sg, rg, sgf, rgf,
    syp, ryp, sy, ry, sdp, rdp, sd, rd, sv, rv, sm, rm, sz, rz, sr, rr,
):
    dp = lax.axis_index("dp")
    ex = lax.axis_index("expert")
    px, py = dp % 4, dp // 4
    core = ex % 2
    other = 1 - core
    group = ex // 4
    partner = (dp, ex + 1 - 2 * core)

    def gray(v):
        return v + (v // 2) * (1 - 2 * (v % 2))

    def to_dp(k):
        return ((py + gray(k // 4)) % 4) * 4 + (px + gray(k % 4)) % 4

    def from_dp(k):
        return ((py + 4 - gray(k // 4)) % 4) * 4 + (px + 4 - gray(k % 4)) % 4

    def to_ex(m):
        return (ex + m) % NEX

    def remote(src, dst, ssem, rsem, where):
        return pltpu.make_async_remote_copy(
            src_ref=src, dst_ref=dst, send_sem=ssem, recv_sem=rsem,
            device_id=where, device_id_type=MESH,
        )

    def cp_gz(m):
        e2 = to_ex(m)
        return remote(gloc.at[e2 % 2], gall.at[ex], sgz.at[m], rgz.at[m], (dp, e2))

    def cp_x(k):
        return remote(xs.at[k], xr.at[core, k], sx.at[k], rx.at[k], (to_dp(k), ex))

    def cp_xf(q):
        half = xr.at[core, pl.ds(q * 4, 4)]
        return remote(half, half, sxf.at[q], rxf.at[q], partner)

    def cp_w(k):
        return remote(ws.at[k], wr.at[k], sw.at[k], rw.at[k], (to_dp(k), ex))

    def cp_g(k):
        return remote(gs.at[k], gr.at[core, k], sg.at[k], rg.at[k], (to_dp(k), ex))

    def cp_gf(q):
        half = gr.at[core, pl.ds(q * 4, 4)]
        return remote(half, half, sgf.at[q], rgf.at[q], partner)

    def cp_yp(q):
        at = pl.ds(q * 4, 4)
        return remote(ypo.at[at], ypi.at[at], syp.at[q], ryp.at[q], partner)

    def cp_y(k):
        return remote(yo.at[k], yret.at[k], sy.at[k], ry.at[k], (from_dp(k), ex))

    def cp_dp(q):
        at = pl.ds(q * 4, 4)
        return remote(dpo.at[at], dpi.at[at], sdp.at[q], rdp.at[q], partner)

    def cp_d(k):
        return remote(do.at[k], dret.at[k], sd.at[k], rd.at[k], (from_dp(k), ex))

    def cp_v(k):
        return remote(vs.at[k], vret.at[k], sv.at[k], rv.at[k], (from_dp(k), ex))

    def cp_m(m):
        e2 = to_ex(m)
        return remote(mst.at[e2], mrecv.at[ex], sm.at[m], rm.at[m], (dp, e2))

    def cp_z(m):
        e2 = to_ex(m)
        return remote(dst_.at[e2], drecv.at[ex], sz.at[m], rz.at[m], (dp, e2))

    def cp_r(m):
        e2 = to_ex(m)
        return remote(rst.at[e2 // 4], rrecv.at[ex], sr.at[m], rr.at[m], (dp, e2))

    def loop(lo, hi, fn):
        def step(i, carry):
            fn(i)
            return carry

        lax.fori_loop(lo, hi, step, 0)

    loads = [
        pltpu.make_async_copy(g_hbm.at[:, pl.ds(0, HALF)], gloc.at[0], in_sem.at[0]),
        pltpu.make_async_copy(g_hbm.at[:, pl.ds(HALF, HALF)], gloc.at[1], in_sem.at[1]),
        pltpu.make_async_copy(tok_hbm.at[:, pl.ds(pl.multiple_of(core * HALF, HALF), HALF)], tok, in_sem.at[2]),
        pltpu.make_async_copy(wg_hbm.at[0], wg, in_sem.at[3]),
        pltpu.make_async_copy(wu_hbm.at[0], wu, in_sem.at[4]),
        pltpu.make_async_copy(wd_hbm.at[0], wd, in_sem.at[5]),
    ]
    for load in loads:
        load.start()

    barrier = pltpu.get_barrier_semaphore()

    def greet(k):
        pl.semaphore_signal(barrier, inc=1, device_id=(to_dp(k), ex), device_id_type=MESH)
        pl.semaphore_signal(barrier, inc=1, device_id=(dp, to_ex(k)), device_id_type=MESH)

    loop(1, NDP, greet)

    def find(k):
        named = routes_ref[...] == to_dp(k) * 4 + group
        hits[pl.ds(k, 1), :] = jnp.sum(named.astype(F32), axis=0, keepdims=True)
        wtok[pl.ds(k, 1), :] = jnp.sum(jnp.where(named, weight_ref[...], 0.0), axis=0, keepdims=True)

    loop(0, NDP, find)
    before = lax.broadcasted_iota(jnp.int32, (TOK, TOK), 0) < lax.broadcasted_iota(jnp.int32, (TOK, TOK), 1)
    ranks = nn(hits[...].astype(BF16), before.astype(F32).astype(BF16))
    rank[...] = jnp.where(hits[...] > 0.5, ranks, -1.0)

    loads[0].wait()
    loads[1].wait()
    pl.semaphore_wait(barrier, 2 * (NDP - 1))
    loop(1, NEX, lambda m: cp_gz(m).start())
    gall[pl.ds(ex, 1)] = gloc[pl.ds(core, 1)]
    loads[2].wait()

    eye = (
        lax.broadcasted_iota(jnp.int32, (CAP, 128), 0) == lax.broadcasted_iota(jnp.int32, (CAP, 128), 1)
    ).astype(F32)

    def to_row(col):
        return jnp.broadcast_to(jnp.sum(eye * col, axis=0, keepdims=True), (8, 128))

    def to_col(row):
        return jnp.sum(eye * row, axis=1, keepdims=True)

    def pick(k):
        slot = lax.broadcasted_iota(jnp.int32, (CAP, TOK), 0).astype(F32)
        hot = (slot == rank[pl.ds(k, 1), :]).astype(F32)
        s = hot.astype(BF16)
        sel[pl.ds(k, 1)] = s.reshape(1, T8, 8, TOK)
        x = nn(s, tok[...]).astype(BF16).reshape(1, T8, 8, HALF)
        w = jnp.sum(hot * wtok[pl.ds(k, 1), :], axis=1, keepdims=True)
        return x, to_row(w)[None]

    def send_x(k):
        x, w = pick(k)
        xs[pl.ds(k, 1)] = x
        ws[pl.ds(k, 1)] = w
        cp_x(k).start()
        cp_w(k).start()

    x0, w0 = pick(0)
    xr[pl.ds(core, 1), 0:1] = x0[None]
    wr[0:1] = w0
    loop(1, NDP, send_x)

    loop(1, NEX, lambda m: cp_gz(m).wait_recv())

    def g_chunk(k):
        return nn(rows_of(sel[pl.ds(k, 1)]), rows_of(gall[...])).astype(BF16).reshape(1, T8, 8, HALF)

    def send_g(k):
        gs[pl.ds(k, 1)] = g_chunk(k)
        cp_g(k).start()

    def got_x(k):
        cp_x(k).wait_recv()
        cp_w(k).wait_recv()

    def pass_x(q):
        loop(jnp.maximum(q * 4, 1), q * 4 + 4, got_x)
        cp_xf(q).start()
        loop(jnp.maximum(q * 4, 1), q * 4 + 4, send_g)

    gr[pl.ds(core, 1), 0:1] = g_chunk(0)[None]
    for load in loads[3:]:
        load.wait()

    def weight_col(q):
        return jnp.concatenate([to_col(wr[pl.ds(q * 4 + r, 1)][0, 0:1]) for r in range(4)], axis=0)

    def forward(q):
        cp_xf(q).wait_recv()
        at = pl.ds(q * 4, 4)
        x0 = rows_of(xr[0, at])
        x1 = rows_of(xr[1, at])
        gate = nt(x0, wg[:, :HALF]) + nt(x1, wg[:, HALF:])
        up = nt(x0, wu[:, :HALF]) + nt(x1, wu[:, HALF:])
        gate_s[q] = gate
        up_s[q] = up
        hidden = gate * jax.nn.sigmoid(gate) * up
        hw = (weight_col(q) * hidden).astype(BF16)
        hwt[q] = hw.T
        send = pl.multiple_of(other * HALF, HALF)
        keep = pl.multiple_of(core * HALF, HALF)
        ypo[at] = nn(hw, wd[:, pl.ds(send, HALF)]).astype(BF16).reshape(4, T8, 8, HALF)
        cp_yp(q).start()
        yo[at] = nn(hw, wd[:, pl.ds(keep, HALF)]).astype(BF16).reshape(4, T8, 8, HALF)

    def return_y(q):
        cp_yp(q).wait_recv()
        at = pl.ds(q * 4, 4)
        yo[at] = (yo[at].astype(F32) + ypi[at].astype(F32)).astype(BF16)
        loop(jnp.maximum(q * 4, 1), q * 4 + 4, lambda k: cp_y(k).start())

    def forward_step(q):
        @pl.when(q < 4)
        def _():
            pass_x(q)

        @pl.when((q >= 1) & (q < 5))
        def _():
            forward(q - 1)

        @pl.when(q >= 2)
        def _():
            return_y(q - 2)

    loop(0, 6, forward_step)
    yret[0:1] = yo[0:1]

    def pass_g(q):
        loop(jnp.maximum(q * 4, 1), q * 4 + 4, lambda k: cp_g(k).wait_recv())
        cp_gf(q).start()

    def backward(q):
        cp_gf(q).wait_recv()
        at = pl.ds(q * 4, 4)
        dh = nt(rows_of(gr[0, at]), wd[:, :HALF]) + nt(rows_of(gr[1, at]), wd[:, HALF:])
        gate = gate_s[q]
        up = up_s[q]
        sigma = jax.nn.sigmoid(gate)
        silu = gate * sigma
        slope = sigma * (1.0 + gate * (1.0 - sigma))
        dot = jnp.sum(silu * up * dh, axis=1, keepdims=True)
        for r in range(4):
            vs[pl.ds(q * 4 + r, 1)] = to_row(dot[r * CAP : (r + 1) * CAP])[None]
        loop(jnp.maximum(q * 4, 1), q * 4 + 4, lambda k: cp_v(k).start())
        dh = weight_col(q) * dh
        dg = (dh * up * slope).astype(BF16)
        du = (dh * silu).astype(BF16)
        dgt[q] = dg.T
        dut[q] = du.T
        send = pl.ds(pl.multiple_of(other * HALF, HALF), HALF)
        keep = pl.ds(pl.multiple_of(core * HALF, HALF), HALF)
        dpo[at] = (nn(dg, wg[:, send]) + nn(du, wu[:, send])).astype(BF16).reshape(4, T8, 8, HALF)
        cp_dp(q).start()
        do[at] = (nn(dg, wg[:, keep]) + nn(du, wu[:, keep])).astype(BF16).reshape(4, T8, 8, HALF)

    def return_d(q):
        cp_dp(q).wait_recv()
        at = pl.ds(q * 4, 4)
        do[at] = (do[at].astype(F32) + dpi[at].astype(F32)).astype(BF16)
        loop(jnp.maximum(q * 4, 1), q * 4 + 4, lambda k: cp_d(k).start())

    def backward_step(q):
        @pl.when(q < 4)
        def _():
            pass_g(q)

        @pl.when((q >= 1) & (q < 5))
        def _():
            backward(q - 1)

        @pl.when(q >= 2)
        def _():
            return_d(q - 2)

    loop(0, 6, backward_step)
    dret[0:1] = do[0:1]
    vret[0:1] = vs[0:1]

    def combine(back, stage):
        def part(n):
            cols = pl.ds(pl.multiple_of(n * COLS, COLS), COLS)
            total = tn(rows_of(sel[0:4]), rows_of(back[0:4, :, :, cols]))
            for q in range(1, 4):
                at = slice(q * 4, q * 4 + 4)
                total += tn(rows_of(sel[at]), rows_of(back[at, :, :, cols]))
            stage[:, :, cols] = total.astype(BF16).reshape(NEX, BLK, COLS)

        loop(0, HALF // COLS, part)

    loop(1, NDP, lambda k: cp_y(k).wait_recv())
    combine(yret, mst)
    loop(1, NEX, lambda m: cp_m(m).start())
    mrecv[pl.ds(ex, 1)] = mst[pl.ds(ex, 1)]

    def grads(n):
        h = n // (HALF // COLS)
        cols = pl.ds(pl.multiple_of((n % (HALF // COLS)) * COLS, COLS), COLS)
        outs = pl.ds(pl.multiple_of(n * COLS, COLS), COLS)

        def total(left, right):
            acc = nn(left[0], rows_of(right[h, 0:4, :, :, cols]))
            for q in range(1, 4):
                acc += nn(left[q], rows_of(right[h, q * 4 : q * 4 + 4, :, :, cols]))
            return acc.astype(BF16)

        gd[:, outs] = total(hwt, gr)
        gg[:, outs] = total(dgt, xr)
        gu[:, outs] = total(dut, xr)

    loop(0, D // COLS, grads)
    stores = [
        pltpu.make_async_copy(gg, gg_hbm.at[0], out_sem.at[0]),
        pltpu.make_async_copy(gu, gu_hbm.at[0], out_sem.at[1]),
        pltpu.make_async_copy(gd, gd_hbm.at[0], out_sem.at[2]),
    ]
    for store in stores:
        store.start()

    rst[...] = jnp.zeros_like(rst)
    loop(1, NDP, lambda k: cp_v(k).wait_recv())

    def route_grad(k):
        col = to_col(vret[pl.ds(k, 1)][0, 0:1])
        row = jnp.sum(rows_of(sel[pl.ds(k, 1)]).astype(F32) * col, axis=0, keepdims=True)
        add = jnp.where(routes_ref[...] == to_dp(k) * 4 + group, row, 0.0)
        for b in range(4):
            rst[b] += add[:, b * 128 : (b + 1) * 128]

    loop(0, NDP, route_grad)
    loop(1, NEX, lambda m: cp_r(m).start())
    rrecv[pl.ds(ex, 1)] = rst[pl.ds(group, 1)]

    loop(1, NDP, lambda k: cp_d(k).wait_recv())
    combine(dret, dst_)
    loop(1, NEX, lambda m: cp_z(m).start())
    drecv[pl.ds(ex, 1)] = dst_[pl.ds(ex, 1)]

    def finish(recv, out):
        for h in range(2):
            total = recv[h].astype(F32)
            for zz in range(1, 8):
                total += recv[zz * 2 + h].astype(F32)
            out[:, h * HALF : (h + 1) * HALF] = total.astype(BF16)

    loop(1, NEX, lambda m: cp_m(m).wait_recv())
    finish(mrecv, mixed_ref)
    loop(1, NEX, lambda m: cp_r(m).wait_recv())
    route_total = jnp.sum(rrecv[...], axis=0)
    mine = (
        lax.broadcasted_iota(jnp.int32, (BLK, 128), 1)
        == lax.broadcasted_iota(jnp.int32, (BLK, 128), 0) + (ex % 4) * BLK
    ).astype(F32)
    lane = lax.broadcasted_iota(jnp.int32, (BLK, 128), 1)
    placed = jnp.zeros((BLK, 128), F32)
    for kk in range(TOP):
        col = jnp.sum(mine * route_total[kk : kk + 1], axis=1, keepdims=True)
        placed = jnp.where(lane == kk, col, placed)
    grw_ref[...] = placed[:, :TOP]
    loop(1, NEX, lambda m: cp_z(m).wait_recv())
    finish(drecv, dx_ref)

    def sent_dp(k):
        cp_x(k).wait_send()
        cp_w(k).wait_send()
        cp_g(k).wait_send()
        cp_y(k).wait_send()
        cp_d(k).wait_send()
        cp_v(k).wait_send()
        cp_gz(k).wait_send()
        cp_m(k).wait_send()
        cp_z(k).wait_send()
        cp_r(k).wait_send()

    loop(1, NDP, sent_dp)

    def sent_q(q):
        cp_xf(q).wait_send()
        cp_gf(q).wait_send()
        cp_yp(q).wait_send()
        cp_dp(q).wait_send()

    loop(0, 4, sent_q)
    for store in stores:
        store.wait()


def body(tokens, routes, route_weight, w_gate, w_up, w_down, grad_out):
    routes_t = jnp.pad(routes.T, ((0, 2), (0, 0)), constant_values=-1)
    weight_t = jnp.pad(route_weight.T, ((0, 2), (0, 0)))
    any_ = pl.BlockSpec(memory_space=pl.ANY)
    vmem = pl.BlockSpec(memory_space=pltpu.VMEM)
    chunk = (NDP, T8, 8, HALF)
    dma = pltpu.SemaphoreType.DMA
    V = pltpu.VMEM
    mixed, dx, grw, gg, gu, gd = pl.pallas_call(
        kernel,
        out_shape=(
            jax.ShapeDtypeStruct((BLK, D), BF16),
            jax.ShapeDtypeStruct((BLK, D), BF16),
            jax.ShapeDtypeStruct((BLK, TOP), F32),
            jax.ShapeDtypeStruct((1, FF, D), BF16),
            jax.ShapeDtypeStruct((1, FF, D), BF16),
            jax.ShapeDtypeStruct((1, FF, D), BF16),
        ),
        in_specs=[any_, vmem, vmem, any_, any_, any_, any_],
        out_specs=(vmem, vmem, vmem, any_, any_, any_),
        scratch_shapes=[
            V((TOK, HALF), BF16), V((2, BLK, HALF), BF16), V((NEX, BLK, HALF), BF16),
            V((FF, D), BF16), V((FF, D), BF16), V((FF, D), BF16),
            V((NDP, TOK), F32), V((NDP, TOK), F32), V((NDP, TOK), F32), V((NDP, T8, 8, TOK), BF16),
            V(chunk, BF16), V((2,) + chunk, BF16), V(chunk, BF16), V((2,) + chunk, BF16),
            V((NDP, 8, 128), F32), V((NDP, 8, 128), F32), V((NDP, 8, 128), F32), V((NDP, 8, 128), F32),
            V(chunk, BF16), V(chunk, BF16), V(chunk, BF16), V(chunk, BF16),
            V(chunk, BF16), V(chunk, BF16), V(chunk, BF16), V(chunk, BF16),
            V((4, ROWS, FF), F32), V((4, ROWS, FF), F32),
            V((4, FF, ROWS), BF16), V((4, FF, ROWS), BF16), V((4, FF, ROWS), BF16),
            V((NEX, BLK, HALF), BF16), V((NEX, BLK, HALF), BF16), V((NEX, BLK, HALF), BF16), V((NEX, BLK, HALF), BF16),
            V((4, 8, 128), F32), V((NEX, 8, 128), F32),
            V((FF, D), BF16), V((FF, D), BF16), V((FF, D), BF16),
            dma((6,)), dma((3,)),
            dma((16,)), dma((16,)), dma((16,)), dma((16,)), dma((4,)), dma((4,)),
            dma((16,)), dma((16,)), dma((16,)), dma((16,)), dma((4,)), dma((4,)),
            dma((4,)), dma((4,)), dma((16,)), dma((16,)), dma((4,)), dma((4,)),
            dma((16,)), dma((16,)), dma((16,)), dma((16,)),
            dma((16,)), dma((16,)), dma((16,)), dma((16,)), dma((16,)), dma((16,)),
        ],
        compiler_params=pltpu.CompilerParams(
            collective_id=0, has_side_effects=True, vmem_limit_bytes=63_000_000
        ),
    )(tokens, routes_t, weight_t, w_gate, w_up, w_down, grad_out)
    return mixed, dx, grw, gg, gu, gd


def solution(mesh):
    rows = P(("dp", "expert"), None)
    block = P(("dp", "expert"), None, None)
    return jax.shard_map(
        body,
        mesh=mesh,
        in_specs=(P("dp", None), P("dp", None), P("dp", None), block, block, block, rows),
        out_specs=(rows, rows, rows, block, block, block),
        check_vma=False,
    )
```

```python
import jax
import jax.numpy as jnp
from jax import lax
from jax.experimental import pallas as pl
from jax.experimental.pallas import tpu as pltpu
from jax.sharding import PartitionSpec as P

MESH = pl.DeviceIdType.MESH
F32 = jnp.float32
BF16 = jnp.bfloat16

TOK = 512
D = 2048
HALF = 1024
FF = 352
TOP = 6
CAP = 72
T8 = CAP // 8
NDP = 16
NEX = 16
BLK = TOK // NEX
ROWS = 4 * CAP
COLS = 512
QUART = 512
PH = 4
PCOL = HALF // PH


def rows_of(ref_value):
    return ref_value.reshape(-1, ref_value.shape[-1])


def nt(a, b):
    return lax.dot_general(a, b, (((1,), (1,)), ((), ())), preferred_element_type=F32)


def tn(a, b):
    return lax.dot_general(a, b, (((0,), (0,)), ((), ())), preferred_element_type=F32)


def nn(a, b):
    return jnp.dot(a, b, preferred_element_type=F32)


def kernel(
    tok_hbm, routes_ref, weight_ref, wg_hbm, wu_hbm, wd_hbm, g_hbm,
    mixed_ref, dx_ref, grw_ref, gg_hbm, gu_hbm, gd_hbm,
    tok, gloc, gall, wg, wu, wd, hits, rank, wtok, sel, selt,
    xs, xr, gs, gr, ws, wr, vs, vret,
    yo, ypi, yzo, yzi, yq, yret, do, dpo, dpi, dret,
    gate_s, up_s, hwt, dgt, dut, dgs, dus,
    mst, mrecv, dst_, drecv, rst, rrecv, gg, gu, gd,
    in_sem, out_sem, sgz, rgz, sx, rx, sxf, rxf, sw, rw, sg, rg, sgf, rgf,
    syp, ryp, syz, ryz, sy, ry, sdp, rdp, sd, rd, sv, rv, sm, rm, sz, rz, sr, rr,
):
    dp = lax.axis_index("dp")
    ex = lax.axis_index("expert")
    px, py = dp % 4, dp // 4
    core = ex % 2
    other = 1 - core
    group = ex // 4
    partner = (dp, ex + 1 - 2 * core)
    odd = (ex // 2) % 2
    across = (dp, ex + 2 - 4 * odd)

    def gray(v):
        return v + (v // 2) * (1 - 2 * (v % 2))

    def to_dp(k):
        return ((py + gray(k // 4)) % 4) * 4 + (px + gray(k % 4)) % 4

    def from_dp(k):
        return ((py + 4 - gray(k // 4)) % 4) * 4 + (px + 4 - gray(k % 4)) % 4

    def to_ex(m):
        return (ex + m) % NEX

    def remote(src, dst, ssem, rsem, where):
        return pltpu.make_async_remote_copy(
            src_ref=src, dst_ref=dst, send_sem=ssem, recv_sem=rsem,
            device_id=where, device_id_type=MESH,
        )

    def cp_gz(m):
        e2 = to_ex(m)
        return remote(gloc.at[e2 % 2], gall.at[ex], sgz.at[0], rgz.at[0], (dp, e2))

    def many_gz():
        return remote(gall.at[pl.ds(0, 15)], gall.at[pl.ds(0, 15)], sgz.at[0], rgz.at[0], partner)

    def many_x(k, n):
        at = pl.ds(k, n)
        return remote(xs.at[at], xr.at[core, at], sx.at[k // 4], rx.at[k // 4], (to_dp(k), ex))

    def cp_xf(q):
        half = xr.at[core, pl.ds(q * 4, 4)]
        return remote(half, half, sxf.at[0], rxf.at[q], partner)

    def many_w(k, n):
        at = pl.ds(k, n)
        return remote(ws.at[at], wr.at[at], sw.at[0], rw.at[k // 4], (to_dp(k), ex))

    def many_g(k, n):
        at = pl.ds(k, n)
        return remote(gs.at[at], gr.at[core, at], sg.at[0], rg.at[k // 4], (to_dp(k), ex))

    def cp_gf(q):
        half = gr.at[core, pl.ds(q * 4, 4)]
        return remote(half, half, sgf.at[0], rgf.at[q], partner)

    def many_yp(q, n):
        at = pl.ds(q * 4, 4 * n)
        return remote(xs.at[at], ypi.at[at], syp.at[0], ryp.at[q], partner)

    def many_yz(q, n):
        at = pl.ds(q * 4, 4 * n)
        return remote(yzo.at[at], yzi.at[at], syz.at[0], ryz.at[q], across)

    def many_y(k, n):
        at = pl.ds(k, n)
        return remote(yq.at[at], yret.at[at], sy.at[0], ry.at[0], (from_dp(k), ex))

    def many_dp(i, n):
        at = pl.ds(i * 4, 4 * n)
        return remote(dpo.at[at], dpi.at[at], sdp.at[0], rdp.at[i], partner)

    def many_d(p, k, n):
        at = pl.ds(p * NDP + k, n)
        return remote(do.at[at], dret.at[at], sd.at[p], rd.at[p], (from_dp(k), ex))

    def many_v(k, n):
        at = pl.ds(k, n)
        return remote(vs.at[at], vret.at[at], sv.at[0], rv.at[0], (from_dp(k), ex))

    def cp_m(m):
        e2 = to_ex(m)
        return remote(mst.at[e2], mrecv.at[ex], sm.at[0], rm.at[0], (dp, e2))

    def many_m():
        return remote(mst.at[pl.ds(0, 15)], mrecv.at[pl.ds(0, 15)], sm.at[0], rm.at[0], partner)

    def cp_z(p, m):
        e2 = to_ex(m)
        return remote(dst_.at[p, e2], drecv.at[p, ex], sz.at[p], rz.at[p], (dp, e2))

    def many_z(p):
        at = pl.ds(0, 15)
        return remote(dst_.at[p, at], drecv.at[p, at], sz.at[p], rz.at[p], partner)

    def cp_r(m):
        e2 = to_ex(m)
        return remote(rst.at[e2 // 4], rrecv.at[ex], sr.at[0], rr.at[0], (dp, e2))

    def many_r():
        at = pl.ds(0, 15)
        return remote(rrecv.at[at], rrecv.at[at], sr.at[0], rr.at[0], partner)

    def by_group(q, fn):
        @pl.when(q == 0)
        def _():
            fn(1, 3)

        @pl.when(q > 0)
        def _():
            fn(q * 4, 4)

    def loop(lo, hi, fn):
        def step(i, carry):
            fn(i)
            return carry

        lax.fori_loop(lo, hi, step, 0)

    loads = [
        pltpu.make_async_copy(g_hbm.at[:, pl.ds(0, HALF)], gloc.at[0], in_sem.at[0]),
        pltpu.make_async_copy(g_hbm.at[:, pl.ds(HALF, HALF)], gloc.at[1], in_sem.at[1]),
        pltpu.make_async_copy(tok_hbm.at[:, pl.ds(pl.multiple_of(core * HALF, HALF), HALF)], tok, in_sem.at[2]),
        pltpu.make_async_copy(wg_hbm.at[0], wg, in_sem.at[3]),
        pltpu.make_async_copy(wu_hbm.at[0], wu, in_sem.at[4]),
        pltpu.make_async_copy(wd_hbm.at[0], wd, in_sem.at[5]),
    ]
    for load in loads:
        load.start()

    barrier = pltpu.get_barrier_semaphore()

    def greet(k):
        pl.semaphore_signal(barrier, inc=1, device_id=(to_dp(k), ex), device_id_type=MESH)
        pl.semaphore_signal(barrier, inc=1, device_id=(dp, to_ex(k)), device_id_type=MESH)

    loop(1, NDP, greet)

    def find(k):
        named = routes_ref[...] == to_dp(k) * 4 + group
        hits[pl.ds(k, 1), :] = jnp.sum(named.astype(F32), axis=0, keepdims=True)
        wtok[pl.ds(k, 1), :] = jnp.sum(jnp.where(named, weight_ref[...], 0.0), axis=0, keepdims=True)

    loop(0, NDP, find)
    before = lax.broadcasted_iota(jnp.int32, (TOK, TOK), 0) < lax.broadcasted_iota(jnp.int32, (TOK, TOK), 1)
    ranks = nn(hits[...].astype(BF16), before.astype(F32).astype(BF16))
    rank[...] = jnp.where(hits[...] > 0.5, ranks, -1.0)

    loads[0].wait()
    loads[1].wait()
    pl.semaphore_wait(barrier, 2 * (NDP - 1))
    loop(1, NEX, lambda m: cp_gz(m).start())
    gall[pl.ds(ex, 1)] = gloc[pl.ds(core, 1)]
    loads[2].wait()

    eye = (
        lax.broadcasted_iota(jnp.int32, (CAP, 128), 0) == lax.broadcasted_iota(jnp.int32, (CAP, 128), 1)
    ).astype(F32)

    def to_row(col):
        return jnp.broadcast_to(jnp.sum(eye * col, axis=0, keepdims=True), (8, 128))

    def to_col(row):
        return jnp.sum(eye * row, axis=1, keepdims=True)

    slot = lax.broadcasted_iota(jnp.int32, (CAP, TOK), 0).astype(F32)

    def send_x(q):
        at = pl.ds(q * 4, 4)
        hot = []
        for r in range(4):
            k = q * 4 + r
            one = (slot == rank[pl.ds(k, 1), :]).astype(F32)
            w = jnp.sum(one * wtok[pl.ds(k, 1), :], axis=1, keepdims=True)
            ws[pl.ds(k, 1)] = to_row(w)[None]
            hot.append(one)
        s = jnp.concatenate(hot, axis=0).astype(BF16)
        sel[at] = s.reshape(4, T8, 8, TOK)
        xs[at] = nn(s, tok[...]).astype(BF16).reshape(4, T8, 8, HALF)

        def go(k):
            many_x(k, 1).start()
            many_w(k, 1).start()

        loop(jnp.maximum(q * 4, 1), q * 4 + 4, go)
        selt[q] = s.T

    loop(0, 4, send_x)
    xr[pl.ds(core, 1), 0:1] = xs[0:1][None]
    wr[0:1] = ws[0:1]

    many_gz().wait_recv()

    def send_g(q):
        at = pl.ds(q * 4, 4)
        gs[at] = nn(rows_of(sel[at]), rows_of(gall[...])).astype(BF16).reshape(4, T8, 8, HALF)
        loop(jnp.maximum(q * 4, 1), q * 4 + 4, lambda k: many_g(k, 1).start())

    def pass_x(q):
        by_group(q, lambda k, n: many_x(k, n).wait_recv())
        by_group(q, lambda k, n: many_w(k, n).wait_recv())
        cp_xf(q).start()

    loop(0, 4, send_g)
    gr[pl.ds(core, 1), 0:1] = gs[0:1][None]
    for load in loads[3:]:
        load.wait()

    def weight_col(q):
        return jnp.concatenate([to_col(wr[pl.ds(q * 4 + r, 1)][0, 0:1]) for r in range(4)], axis=0)

    def forward(q):
        cp_xf(q).wait_recv()
        at = pl.ds(q * 4, 4)
        x0 = rows_of(xr[0, at])
        x1 = rows_of(xr[1, at])
        gate = nt(x0, wg[:, :HALF]) + nt(x1, wg[:, HALF:])
        up = nt(x0, wu[:, :HALF]) + nt(x1, wu[:, HALF:])
        gate_s[q] = gate
        up_s[q] = up
        hidden = gate * jax.nn.sigmoid(gate) * up
        hw = (weight_col(q) * hidden).astype(BF16)
        hwt[q] = hw.T
        send = pl.multiple_of(other * HALF, HALF)
        keep = pl.multiple_of(core * HALF, HALF)
        by_group(q, lambda k, n: many_x(k, n).wait_send())
        xs[at] = nn(hw, wd[:, pl.ds(send, HALF)]).astype(BF16).reshape(4, T8, 8, HALF)
        many_yp(q, 1).start()
        yo[at] = nn(hw, wd[:, pl.ds(keep, HALF)]).astype(BF16).reshape(4, T8, 8, HALF)

    def cross_y(q):
        many_yp(q, 1).wait_recv()
        at = pl.ds(q * 4, 4)
        send = pl.ds(pl.multiple_of((1 - odd) * QUART, QUART), QUART)
        keep = pl.ds(pl.multiple_of(odd * QUART, QUART), QUART)
        yzo[at] = (yo[at, :, :, send].astype(F32) + ypi[at, :, :, send].astype(F32)).astype(BF16)
        many_yz(q, 1).start()
        yq[at] = (yo[at, :, :, keep].astype(F32) + ypi[at, :, :, keep].astype(F32)).astype(BF16)

    def return_y(q):
        many_yz(q, 1).wait_recv()
        at = pl.ds(q * 4, 4)
        yq[at] = (yq[at].astype(F32) + yzi[at].astype(F32)).astype(BF16)
        loop(jnp.maximum(q * 4, 1), q * 4 + 4, lambda k: many_y(k, 1).start())

    def forward_step(q):
        @pl.when(q < 4)
        def _():
            pass_x(q)

        @pl.when((q >= 1) & (q < 5))
        def _():
            forward(q - 1)

        @pl.when((q >= 2) & (q < 6))
        def _():
            cross_y(q - 2)

        @pl.when(q >= 3)
        def _():
            return_y(q - 3)

    loop(0, 7, forward_step)
    yret[0:1] = yq[0:1]

    def pass_g(q):
        by_group(q, lambda k, n: many_g(k, n).wait_recv())
        cp_gf(q).start()

    def backward(q):
        cp_gf(q).wait_recv()
        at = pl.ds(q * 4, 4)
        dh = nt(rows_of(gr[0, at]), wd[:, :HALF]) + nt(rows_of(gr[1, at]), wd[:, HALF:])
        gate = gate_s[q]
        up = up_s[q]
        sigma = jax.nn.sigmoid(gate)
        silu = gate * sigma
        slope = sigma * (1.0 + gate * (1.0 - sigma))
        dot = jnp.sum(silu * up * dh, axis=1, keepdims=True)
        for r in range(4):
            vs[pl.ds(q * 4 + r, 1)] = to_row(dot[r * CAP : (r + 1) * CAP])[None]
        loop(jnp.maximum(q * 4, 1), q * 4 + 4, lambda k: many_v(k, 1).start())
        dh = weight_col(q) * dh
        dg = (dh * up * slope).astype(BF16)
        du = (dh * silu).astype(BF16)
        dgt[q] = dg.T
        dut[q] = du.T
        dgs[q] = dg
        dus[q] = du

    def backward_step(q):
        @pl.when(q < 4)
        def _():
            pass_g(q)

        @pl.when(q >= 1)
        def _():
            backward(q - 1)

    loop(0, 5, backward_step)

    def input_grad(i):
        p, q = i // 4, i % 4
        at = pl.ds(i * 4, 4)
        send = pl.ds(pl.multiple_of(other * HALF + p * PCOL, PCOL), PCOL)
        keep = pl.ds(pl.multiple_of(core * HALF + p * PCOL, PCOL), PCOL)
        dpo[at] = (nn(dgs[q], wg[:, send]) + nn(dus[q], wu[:, send])).astype(BF16).reshape(4, T8, 8, PCOL)
        many_dp(i, 1).start()
        do[at] = (nn(dgs[q], wg[:, keep]) + nn(dus[q], wu[:, keep])).astype(BF16).reshape(4, T8, 8, PCOL)

    def return_d(i):
        p, q = i // 4, i % 4
        many_dp(i, 1).wait_recv()
        at = pl.ds(i * 4, 4)
        do[at] = (do[at].astype(F32) + dpi[at].astype(F32)).astype(BF16)

        @pl.when(p < 2)
        def _():
            loop(jnp.maximum(q * 4, 1), q * 4 + 4, lambda k: many_d(p, k, 1).start())

    def input_step(i):
        @pl.when(i < 4 * PH)
        def _():
            input_grad(i)

        @pl.when(i >= 1)
        def _():
            return_d(i - 1)

    loop(0, 4 * PH + 1, input_step)
    for p in range(PH):
        dret[p * NDP : p * NDP + 1] = do[p * NDP : p * NDP + 1]
    vret[0:1] = vs[0:1]

    def combine(back, base):
        total = nn(selt[0], rows_of(back[pl.ds(base, 4)]))
        for q in range(1, 4):
            total += nn(selt[q], rows_of(back[pl.ds(base + q * 4, 4)]))
        return total.astype(BF16).reshape(NEX, BLK, back.shape[-1])

    many_y(1, 15).wait_recv()
    mst[...] = combine(yret, 0)
    loop(1, NEX, lambda m: cp_m(m).start())
    mrecv[pl.ds(ex, 1)] = mst[pl.ds(ex, 1)]

    rst[...] = jnp.zeros_like(rst)
    many_v(1, 15).wait_recv()

    def route_grad(k):
        col = to_col(vret[pl.ds(k, 1)][0, 0:1])
        row = jnp.sum(rows_of(sel[pl.ds(k, 1)]).astype(F32) * col, axis=0, keepdims=True)
        add = jnp.where(routes_ref[...] == to_dp(k) * 4 + group, row, 0.0)
        for b in range(4):
            rst[b, :TOP] += add[:, b * 128 : (b + 1) * 128]

    loop(0, NDP, route_grad)
    loop(1, NEX, lambda m: cp_r(m).start())
    rrecv[pl.ds(ex, 1)] = rst[pl.ds(group, 1)]

    def grads(n):
        h = n // (HALF // COLS)
        cols = pl.ds(pl.multiple_of((n % (HALF // COLS)) * COLS, COLS), COLS)
        outs = pl.ds(pl.multiple_of(n * COLS, COLS), COLS)

        def total(left, right):
            acc = nn(left[0], rows_of(right[h, 0:4, :, :, cols]))
            for q in range(1, 4):
                acc += nn(left[q], rows_of(right[h, q * 4 : q * 4 + 4, :, :, cols]))
            return acc.astype(BF16)

        gd[:, outs] = total(hwt, gr)
        gg[:, outs] = total(dgt, xr)
        gu[:, outs] = total(dut, xr)

    def phase(p):
        many_d(p, 1, 15).wait_recv()

        @pl.when(p + 2 < PH)
        def _():
            loop(1, NDP, lambda k: many_d(p + 2, k + core * (NDP - 2 * k), 1).start())

        dst_[pl.ds(p, 1)] = combine(dret, p * NDP)[None]
        loop(1, NEX, lambda m: cp_z(p, m).start())
        drecv[pl.ds(p, 1), pl.ds(ex, 1)] = dst_[pl.ds(p, 1), pl.ds(ex, 1)]
        grads(p)

    loop(0, PH, phase)
    stores = [
        pltpu.make_async_copy(gg, gg_hbm.at[0], out_sem.at[0]),
        pltpu.make_async_copy(gu, gu_hbm.at[0], out_sem.at[1]),
        pltpu.make_async_copy(gd, gd_hbm.at[0], out_sem.at[2]),
    ]
    for store in stores:
        store.start()

    many_m().wait_recv()
    for b in range(4):
        source = (b % 2) * 2 + b // 2
        total = mrecv[source].astype(F32)
        for gg_ in range(1, 4):
            total += mrecv[gg_ * 4 + source].astype(F32)
        mixed_ref[:, b * QUART : (b + 1) * QUART] = total.astype(BF16)
    many_r().wait_recv()
    route_total = jnp.sum(rrecv[...], axis=0)
    mine = jnp.zeros((TOP, BLK), F32)
    for b in range(4):
        mine = jnp.where(ex % 4 == b, route_total[:TOP, b * BLK : (b + 1) * BLK], mine)
    grw_ref[...] = mine
    for p in range(PH):
        many_z(p).wait_recv()
        for h in range(2):
            total = drecv[p, h].astype(F32)
            for zz in range(1, 8):
                total += drecv[p, zz * 2 + h].astype(F32)
            start = h * HALF + p * PCOL
            dx_ref[:, start : start + PCOL] = total.astype(BF16)

    many_gz().wait_send()
    many_w(1, 15).wait_send()
    many_g(1, 15).wait_send()
    cp_all = remote(xr.at[0], xr.at[1], sxf.at[0], rxf.at[0], partner)
    cp_all.wait_send()
    cp_all = remote(gr.at[0], gr.at[1], sgf.at[0], rgf.at[0], partner)
    cp_all.wait_send()
    many_yp(0, 4).wait_send()
    many_yz(0, 4).wait_send()
    many_y(1, 15).wait_send()
    many_dp(0, 4 * PH).wait_send()
    many_v(1, 15).wait_send()
    many_m().wait_send()
    many_r().wait_send()
    for p in range(PH):
        many_d(p, 1, 15).wait_send()
        many_z(p).wait_send()
    for store in stores:
        store.wait()


def hand_over(*refs):
    count = (len(refs) - 2) // 3
    held, (read, write) = refs[2 * count : 3 * count], refs[3 * count :]
    ins = [pltpu.make_async_copy(refs[i], held[i], read.at[i]) for i in range(count)]
    outs = [pltpu.make_async_copy(held[i], refs[count + i], write.at[i]) for i in range(count)]
    for copy in ins:
        copy.start()
    for i in range(count):
        ins[i].wait()
        outs[i].start()
    for copy in outs:
        copy.wait()


def body(tokens, routes, route_weight, w_gate, w_up, w_down, grad_out):
    any_ = pl.BlockSpec(memory_space=pl.ANY)
    vmem = pl.BlockSpec(memory_space=pltpu.VMEM)
    chunk = (NDP, T8, 8, HALF)
    quart = (NDP, T8, 8, QUART)
    phased = (PH * NDP, T8, 8, PCOL)
    dma = pltpu.SemaphoreType.DMA
    V = pltpu.VMEM
    results = pl.pallas_call(
        kernel,
        out_shape=(
            jax.ShapeDtypeStruct((BLK, D), BF16),
            jax.ShapeDtypeStruct((BLK, D), BF16),
            jax.ShapeDtypeStruct((TOP, BLK), F32),
            jax.ShapeDtypeStruct((1, FF, D), BF16),
            jax.ShapeDtypeStruct((1, FF, D), BF16),
            jax.ShapeDtypeStruct((1, FF, D), BF16),
        ),
        in_specs=[any_, vmem, vmem, any_, any_, any_, any_],
        out_specs=(vmem, vmem, vmem, any_, any_, any_),
        scratch_shapes=[
            V((TOK, HALF), BF16), V((2, BLK, HALF), BF16), V((NEX, BLK, HALF), BF16),
            V((FF, D), BF16), V((FF, D), BF16), V((FF, D), BF16),
            V((NDP, TOK), F32), V((NDP, TOK), F32), V((NDP, TOK), F32), V((NDP, T8, 8, TOK), BF16), V((4, TOK, ROWS), BF16),
            V(chunk, BF16), V((2,) + chunk, BF16), V(chunk, BF16), V((2,) + chunk, BF16),
            V((NDP, 8, 128), F32), V((NDP, 8, 128), F32), V((NDP, 8, 128), F32), V((NDP, 8, 128), F32),
            V(chunk, BF16), V(chunk, BF16), V(quart, BF16), V(quart, BF16), V(quart, BF16), V(quart, BF16),
            V(phased, BF16), V(phased, BF16), V(phased, BF16), V(phased, BF16),
            V((4, ROWS, FF), F32), V((4, ROWS, FF), F32),
            V((4, FF, ROWS), BF16), V((4, FF, ROWS), BF16), V((4, FF, ROWS), BF16), V((4, ROWS, FF), BF16), V((4, ROWS, FF), BF16),
            V((NEX, BLK, QUART), BF16), V((NEX, BLK, QUART), BF16), V((PH, NEX, BLK, PCOL), BF16), V((PH, NEX, BLK, PCOL), BF16),
            V((4, 8, 128), F32), V((NEX, 8, 128), F32),
            V((FF, D), BF16), V((FF, D), BF16), V((FF, D), BF16),
            dma((6,)), dma((3,)),
            dma((1,)), dma((1,)), dma((4,)), dma((4,)), dma((1,)), dma((4,)),
            dma((1,)), dma((4,)), dma((1,)), dma((4,)), dma((1,)), dma((4,)),
            dma((1,)), dma((4,)), dma((1,)), dma((4,)), dma((1,)), dma((1,)), dma((1,)), dma((4 * PH,)),
            dma((PH,)), dma((PH,)), dma((1,)), dma((1,)),
            dma((1,)), dma((1,)), dma((PH,)), dma((PH,)), dma((1,)), dma((1,)),
        ],
        compiler_params=pltpu.CompilerParams(
            collective_id=0, has_side_effects=True, vmem_limit_bytes=63_000_000
        ),
    )(tokens, routes.T, route_weight.T, w_gate, w_up, w_down, grad_out)
    mixed, dx, grw, gg, gu, gd = pl.pallas_call(
        hand_over,
        out_shape=tuple(jax.ShapeDtypeStruct(r.shape, r.dtype) for r in results),
        in_specs=[any_] * 6,
        out_specs=(any_,) * 6,
        scratch_shapes=[V(r.shape, r.dtype) for r in results] + [dma((6,)), dma((6,))],
    )(*results)
    return mixed, dx, grw.T, gg, gu, gd


def solution(mesh):
    rows = P(("dp", "expert"), None)
    block = P(("dp", "expert"), None, None)
    return jax.shard_map(
        body,
        mesh=mesh,
        in_specs=(P("dp", None), P("dp", None), P("dp", None), block, block, block, rows),
        out_specs=(rows, rows, rows, block, block, block),
        check_vma=False,
    )
```

```python
import jax
import jax.numpy as jnp
from jax import lax
from jax.experimental import pallas as pl
from jax.experimental.pallas import tpu as pltpu
from jax.sharding import PartitionSpec as P

MESH = pl.DeviceIdType.MESH
F32 = jnp.float32
BF16 = jnp.bfloat16

TOK = 512
D = 2048
HALF = 1024
FF = 352
TOP = 6
CAP = 72
T8 = CAP // 8
NDP = 16
NEX = 16
BLK = TOK // NEX
ROWS = 4 * CAP
COLS = 512
QUART = 512
PH = 4
PCOL = HALF // PH


def rows_of(ref_value):
    return ref_value.reshape(-1, ref_value.shape[-1])


def nt(a, b):
    return lax.dot_general(a, b, (((1,), (1,)), ((), ())), preferred_element_type=F32)


def tn(a, b):
    return lax.dot_general(a, b, (((0,), (0,)), ((), ())), preferred_element_type=F32)


def nn(a, b):
    return jnp.dot(a, b, preferred_element_type=F32)


def kernel(
    tok_hbm, routes_ref, weight_ref, wg_hbm, wu_hbm, wd_hbm, g_hbm,
    mixed_ref, dx_ref, grw_ref, gg_hbm, gu_hbm, gd_hbm,
    tok, gloc, gall, wg, wu, wd, hits, rank, wtok, sel, selt,
    xs, xr, gs, gr, ws, wr, vs, vret,
    yo, ypi, yzo, yzi, yq, yret, do, dpo, dpi, dret,
    gate_s, up_s, hwt, dgt, dut, dgs, dus,
    mst, mrecv, dst_, pre, drecv, rst, rrecv, gg, gu, gd,
    in_sem, out_sem, sgz, rgz, sx, rx, sxf, rxf, sw, rw, sg, rg, sgf, rgf,
    syp, ryp, syz, ryz, sy, ry, sdp, rdp, sd, rd, sv, rv, sm, rm, spre, rpre, sz, rz, sr, rr,
):
    dp = lax.axis_index("dp")
    ex = lax.axis_index("expert")
    px, py = dp % 4, dp // 4
    core = ex % 2
    other = 1 - core
    group = ex // 4
    partner = (dp, ex + 1 - 2 * core)
    ez = ex // 2
    odd = ez % 2
    across = (dp, ex + 2 - 4 * odd)

    def gray(v):
        return v + (v // 2) * (1 - 2 * (v % 2))

    def to_dp(k):
        return ((py + gray(k // 4)) % 4) * 4 + (px + gray(k % 4)) % 4

    def from_dp(k):
        return ((py + 4 - gray(k // 4)) % 4) * 4 + (px + 4 - gray(k % 4)) % 4

    def to_ex(m):
        return (ex + m) % NEX

    def remote(src, dst, ssem, rsem, where):
        return pltpu.make_async_remote_copy(
            src_ref=src, dst_ref=dst, send_sem=ssem, recv_sem=rsem,
            device_id=where, device_id_type=MESH,
        )

    def cp_gz(m):
        e2 = to_ex(m)
        return remote(gloc.at[e2 % 2], gall.at[ex], sgz.at[0], rgz.at[0], (dp, e2))

    def many_gz():
        return remote(gall.at[pl.ds(0, 15)], gall.at[pl.ds(0, 15)], sgz.at[0], rgz.at[0], partner)

    def many_x(k, n):
        at = pl.ds(k, n)
        return remote(xs.at[at], xr.at[core, at], sx.at[k // 4], rx.at[k // 4], (to_dp(k), ex))

    def cp_xf(q):
        half = xr.at[core, pl.ds(q * 4, 4)]
        return remote(half, half, sxf.at[0], rxf.at[q], partner)

    def many_w(k, n):
        at = pl.ds(k, n)
        return remote(ws.at[at], wr.at[at], sw.at[0], rw.at[k // 4], (to_dp(k), ex))

    def many_g(k, n):
        at = pl.ds(k, n)
        return remote(gs.at[at], gr.at[core, at], sg.at[0], rg.at[k // 4], (to_dp(k), ex))

    def cp_gf(q):
        half = gr.at[core, pl.ds(q * 4, 4)]
        return remote(half, half, sgf.at[0], rgf.at[q], partner)

    def many_yp(q, n):
        at = pl.ds(q * 4, 4 * n)
        return remote(xs.at[at], ypi.at[at], syp.at[0], ryp.at[q], partner)

    def many_yz(q, n):
        at = pl.ds(q * 4, 4 * n)
        return remote(yzo.at[at], yzi.at[at], syz.at[0], ryz.at[q], across)

    def many_y(k, n):
        at = pl.ds(k, n)
        return remote(yq.at[at], yret.at[at], sy.at[0], ry.at[0], (from_dp(k), ex))

    def many_dp(i, n):
        at = pl.ds(i * 4, 4 * n)
        return remote(dpo.at[at], dpi.at[at], sdp.at[0], rdp.at[i], partner)

    def many_d(p, k, n):
        at = pl.ds(p * NDP + k, n)
        return remote(do.at[at], dret.at[at], sd.at[p], rd.at[p], (from_dp(k), ex))

    def many_v(k, n):
        at = pl.ds(k, n)
        return remote(vs.at[at], vret.at[at], sv.at[0], rv.at[0], (from_dp(k), ex))

    def cp_m(m):
        e2 = to_ex(m)
        return remote(mst.at[e2], mrecv.at[ex], sm.at[0], rm.at[0], (dp, e2))

    def many_m():
        return remote(mst.at[pl.ds(0, 15)], mrecv.at[pl.ds(0, 15)], sm.at[0], rm.at[0], partner)

    def chip(n, z, c):
        return (z + (1 - 2 * c) * n + 8) % 8

    def cp_pre(p, i, d, to):
        src = dst_.at[p, pl.ds(2 * chip(d, ez, core), 2)]
        return remote(src, pre.at[p, i], spre.at[p], rpre.at[p], (dp, 2 * chip(to, ez, core) + core))

    def many_pre(p):
        return remote(pre.at[p], pre.at[p], spre.at[p], rpre.at[p], partner)

    def cp_z(p, i, d, c2):
        e2 = 2 * chip(d, ez, core) + c2
        return remote(dst_.at[p, e2], drecv.at[p, core * 5 + i], sz.at[p], rz.at[p], (dp, e2))

    def many_z(p):
        at = pl.ds(0, 9)
        return remote(drecv.at[p, at], drecv.at[p, at], sz.at[p], rz.at[p], partner)

    def cp_r(m):
        e2 = to_ex(m)
        return remote(rst.at[e2 // 4], rrecv.at[ex], sr.at[0], rr.at[0], (dp, e2))

    def many_r():
        at = pl.ds(0, 15)
        return remote(rrecv.at[at], rrecv.at[at], sr.at[0], rr.at[0], partner)

    def by_group(q, fn):
        @pl.when(q == 0)
        def _():
            fn(1, 3)

        @pl.when(q > 0)
        def _():
            fn(q * 4, 4)

    def loop(lo, hi, fn):
        def step(i, carry):
            fn(i)
            return carry

        lax.fori_loop(lo, hi, step, 0)

    loads = [
        pltpu.make_async_copy(g_hbm.at[:, pl.ds(0, HALF)], gloc.at[0], in_sem.at[0]),
        pltpu.make_async_copy(g_hbm.at[:, pl.ds(HALF, HALF)], gloc.at[1], in_sem.at[1]),
        pltpu.make_async_copy(tok_hbm.at[:, pl.ds(pl.multiple_of(core * HALF, HALF), HALF)], tok, in_sem.at[2]),
        pltpu.make_async_copy(wg_hbm.at[0], wg, in_sem.at[3]),
        pltpu.make_async_copy(wu_hbm.at[0], wu, in_sem.at[4]),
        pltpu.make_async_copy(wd_hbm.at[0], wd, in_sem.at[5]),
    ]
    for load in loads:
        load.start()

    barrier = pltpu.get_barrier_semaphore()

    def greet(k):
        pl.semaphore_signal(barrier, inc=1, device_id=(to_dp(k), ex), device_id_type=MESH)
        pl.semaphore_signal(barrier, inc=1, device_id=(dp, to_ex(k)), device_id_type=MESH)

    loop(1, NDP, greet)

    def find(k):
        named = routes_ref[...] == to_dp(k) * 4 + group
        hits[pl.ds(k, 1), :] = jnp.sum(named.astype(F32), axis=0, keepdims=True)
        wtok[pl.ds(k, 1), :] = jnp.sum(jnp.where(named, weight_ref[...], 0.0), axis=0, keepdims=True)

    loop(0, NDP, find)
    before = lax.broadcasted_iota(jnp.int32, (TOK, TOK), 0) < lax.broadcasted_iota(jnp.int32, (TOK, TOK), 1)
    ranks = nn(hits[...].astype(BF16), before.astype(F32).astype(BF16))
    rank[...] = jnp.where(hits[...] > 0.5, ranks, -1.0)

    loads[0].wait()
    loads[1].wait()
    pl.semaphore_wait(barrier, 2 * (NDP - 1))
    loop(1, NEX, lambda m: cp_gz(m).start())
    gall[pl.ds(ex, 1)] = gloc[pl.ds(core, 1)]
    loads[2].wait()

    eye = (
        lax.broadcasted_iota(jnp.int32, (CAP, 128), 0) == lax.broadcasted_iota(jnp.int32, (CAP, 128), 1)
    ).astype(F32)

    def to_row(col):
        return jnp.broadcast_to(jnp.sum(eye * col, axis=0, keepdims=True), (8, 128))

    def to_col(row):
        return jnp.sum(eye * row, axis=1, keepdims=True)

    slot = lax.broadcasted_iota(jnp.int32, (CAP, TOK), 0).astype(F32)

    def send_x(q):
        at = pl.ds(q * 4, 4)
        hot = []
        for r in range(4):
            k = q * 4 + r
            one = (slot == rank[pl.ds(k, 1), :]).astype(F32)
            w = jnp.sum(one * wtok[pl.ds(k, 1), :], axis=1, keepdims=True)
            ws[pl.ds(k, 1)] = to_row(w)[None]
            hot.append(one)
        s = jnp.concatenate(hot, axis=0).astype(BF16)
        sel[at] = s.reshape(4, T8, 8, TOK)
        xs[at] = nn(s, tok[...]).astype(BF16).reshape(4, T8, 8, HALF)

        def go(k):
            many_x(k, 1).start()
            many_w(k, 1).start()

        loop(jnp.maximum(q * 4, 1), q * 4 + 4, go)
        selt[q] = s.T

    loop(0, 4, send_x)
    xr[pl.ds(core, 1), 0:1] = xs[0:1][None]
    wr[0:1] = ws[0:1]

    many_gz().wait_recv()

    def send_g(q):
        at = pl.ds(q * 4, 4)
        gs[at] = nn(rows_of(sel[at]), rows_of(gall[...])).astype(BF16).reshape(4, T8, 8, HALF)
        loop(jnp.maximum(q * 4, 1), q * 4 + 4, lambda k: many_g(k, 1).start())

    def pass_x(q):
        by_group(q, lambda k, n: many_x(k, n).wait_recv())
        by_group(q, lambda k, n: many_w(k, n).wait_recv())
        cp_xf(q).start()

    loop(0, 4, send_g)
    gr[pl.ds(core, 1), 0:1] = gs[0:1][None]
    for load in loads[3:]:
        load.wait()

    def weight_col(q):
        return jnp.concatenate([to_col(wr[pl.ds(q * 4 + r, 1)][0, 0:1]) for r in range(4)], axis=0)

    def forward(q):
        cp_xf(q).wait_recv()
        at = pl.ds(q * 4, 4)
        x0 = rows_of(xr[0, at])
        x1 = rows_of(xr[1, at])
        gate = nt(x0, wg[:, :HALF]) + nt(x1, wg[:, HALF:])
        up = nt(x0, wu[:, :HALF]) + nt(x1, wu[:, HALF:])
        gate_s[q] = gate
        up_s[q] = up
        hidden = gate * jax.nn.sigmoid(gate) * up
        hw = (weight_col(q) * hidden).astype(BF16)
        hwt[q] = hw.T
        send = pl.multiple_of(other * HALF, HALF)
        keep = pl.multiple_of(core * HALF, HALF)
        by_group(q, lambda k, n: many_x(k, n).wait_send())
        xs[at] = nn(hw, wd[:, pl.ds(send, HALF)]).astype(BF16).reshape(4, T8, 8, HALF)
        many_yp(q, 1).start()
        yo[at] = nn(hw, wd[:, pl.ds(keep, HALF)]).astype(BF16).reshape(4, T8, 8, HALF)

    def cross_y(q):
        many_yp(q, 1).wait_recv()
        at = pl.ds(q * 4, 4)
        send = pl.ds(pl.multiple_of((1 - odd) * QUART, QUART), QUART)
        keep = pl.ds(pl.multiple_of(odd * QUART, QUART), QUART)
        yzo[at] = (yo[at, :, :, send].astype(F32) + ypi[at, :, :, send].astype(F32)).astype(BF16)
        many_yz(q, 1).start()
        yq[at] = (yo[at, :, :, keep].astype(F32) + ypi[at, :, :, keep].astype(F32)).astype(BF16)

    def return_y(q):
        many_yz(q, 1).wait_recv()
        at = pl.ds(q * 4, 4)
        yq[at] = (yq[at].astype(F32) + yzi[at].astype(F32)).astype(BF16)
        loop(jnp.maximum(q * 4, 1), q * 4 + 4, lambda k: many_y(k, 1).start())

    def forward_step(q):
        @pl.when(q < 4)
        def _():
            pass_x(q)

        @pl.when((q >= 1) & (q < 5))
        def _():
            forward(q - 1)

        @pl.when((q >= 2) & (q < 6))
        def _():
            cross_y(q - 2)

        @pl.when(q >= 3)
        def _():
            return_y(q - 3)

    loop(0, 7, forward_step)
    yret[0:1] = yq[0:1]

    def pass_g(q):
        by_group(q, lambda k, n: many_g(k, n).wait_recv())
        cp_gf(q).start()

    def backward(q):
        cp_gf(q).wait_recv()
        at = pl.ds(q * 4, 4)
        dh = nt(rows_of(gr[0, at]), wd[:, :HALF]) + nt(rows_of(gr[1, at]), wd[:, HALF:])
        gate = gate_s[q]
        up = up_s[q]
        sigma = jax.nn.sigmoid(gate)
        silu = gate * sigma
        slope = sigma * (1.0 + gate * (1.0 - sigma))
        dot = jnp.sum(silu * up * dh, axis=1, keepdims=True)
        for r in range(4):
            vs[pl.ds(q * 4 + r, 1)] = to_row(dot[r * CAP : (r + 1) * CAP])[None]
        loop(jnp.maximum(q * 4, 1), q * 4 + 4, lambda k: many_v(k, 1).start())
        dh = weight_col(q) * dh
        dg = (dh * up * slope).astype(BF16)
        du = (dh * silu).astype(BF16)
        dgt[q] = dg.T
        dut[q] = du.T
        dgs[q] = dg
        dus[q] = du

    def backward_step(q):
        @pl.when(q < 4)
        def _():
            pass_g(q)

        @pl.when(q >= 1)
        def _():
            backward(q - 1)

    loop(0, 5, backward_step)

    def input_grad(i):
        p, q = i // 4, i % 4
        at = pl.ds(i * 4, 4)
        send = pl.ds(pl.multiple_of(other * HALF + p * PCOL, PCOL), PCOL)
        keep = pl.ds(pl.multiple_of(core * HALF + p * PCOL, PCOL), PCOL)
        dpo[at] = (nn(dgs[q], wg[:, send]) + nn(dus[q], wu[:, send])).astype(BF16).reshape(4, T8, 8, PCOL)
        many_dp(i, 1).start()
        do[at] = (nn(dgs[q], wg[:, keep]) + nn(dus[q], wu[:, keep])).astype(BF16).reshape(4, T8, 8, PCOL)

    def return_d(i):
        p, q = i // 4, i % 4
        many_dp(i, 1).wait_recv()
        at = pl.ds(i * 4, 4)
        do[at] = (do[at].astype(F32) + dpi[at].astype(F32)).astype(BF16)

        @pl.when(p < 1)
        def _():
            loop(jnp.maximum(q * 4, 1), q * 4 + 4, lambda k: many_d(p, k, 1).start())

    def input_step(i):
        @pl.when(i < 4 * PH)
        def _():
            input_grad(i)

        @pl.when(i >= 1)
        def _():
            return_d(i - 1)

    loop(0, 4 * PH + 1, input_step)
    for p in range(PH):
        dret[p * NDP : p * NDP + 1] = do[p * NDP : p * NDP + 1]
    vret[0:1] = vs[0:1]

    def combine(back, base):
        total = nn(selt[0], rows_of(back[pl.ds(base, 4)]))
        for q in range(1, 4):
            total += nn(selt[q], rows_of(back[pl.ds(base + q * 4, 4)]))
        return total.astype(BF16).reshape(NEX, BLK, back.shape[-1])

    def go_d(p):
        loop(1, NDP, lambda k: many_d(p, k + core * (NDP - 2 * k), 1).start())

    many_y(1, 15).wait_recv()
    go_d(1)
    mst[...] = combine(yret, 0)
    loop(1, NEX, lambda m: cp_m(m).start())
    mrecv[pl.ds(ex, 1)] = mst[pl.ds(ex, 1)]

    rst[...] = jnp.zeros_like(rst)
    many_v(1, 15).wait_recv()

    def route_grad(k):
        col = to_col(vret[pl.ds(k, 1)][0, 0:1])
        row = jnp.sum(rows_of(sel[pl.ds(k, 1)]).astype(F32) * col, axis=0, keepdims=True)
        add = jnp.where(routes_ref[...] == to_dp(k) * 4 + group, row, 0.0)
        for b in range(4):
            rst[b, :TOP] += add[:, b * 128 : (b + 1) * 128]

    loop(0, NDP, route_grad)
    loop(1, NEX, lambda m: cp_r(m).start())
    rrecv[pl.ds(ex, 1)] = rst[pl.ds(group, 1)]

    def grads(n):
        h = n // (HALF // COLS)
        cols = pl.ds(pl.multiple_of((n % (HALF // COLS)) * COLS, COLS), COLS)
        outs = pl.ds(pl.multiple_of(n * COLS, COLS), COLS)

        def total(left, right):
            acc = nn(left[0], rows_of(right[h, 0:4, :, :, cols]))
            for q in range(1, 4):
                acc += nn(left[q], rows_of(right[h, q * 4 : q * 4 + 4, :, :, cols]))
            return acc.astype(BF16)

        gd[:, outs] = total(hwt, gr)
        gg[:, outs] = total(dgt, xr)
        gu[:, outs] = total(dut, xr)

    def arrive(p):
        many_d(p, 1, 15).wait_recv()

        @pl.when(p + 2 < PH)
        def _():
            go_d(p + 2)

        dst_[pl.ds(p, 1)] = combine(dret, p * NDP)[None]
        cp_pre(p, 0, -4, -1).start()
        cp_pre(p, 1, -2, -1).start()
        cp_pre(p, 2, 3, 1).start()
        cp_z(p, 3, 1, 0).start()
        cp_z(p, 3, 1, 1).start()
        cp_z(p, 4, 0, other).start()
        drecv[pl.ds(p, 1), pl.ds(core * 5 + 4, 1)] = dst_[pl.ds(p, 1), pl.ds(ex, 1)]
        grads(p)

    def pass_on(p):
        many_pre(p).wait_recv()
        for i, d in ((0, -3), (1, -1), (2, 2)):
            at = pl.ds(2 * chip(d, ez, core), 2)
            joined = dst_[pl.ds(p, 1), at].astype(F32) + pre[pl.ds(p, 1), i].astype(F32)
            dst_[pl.ds(p, 1), at] = joined.astype(BF16)
            cp_z(p, i, d, 0).start()
            cp_z(p, i, d, 1).start()

    def phase(p):
        @pl.when(p < PH)
        def _():
            arrive(p)

        @pl.when(p >= 1)
        def _():
            pass_on(p - 1)

    loop(0, PH + 1, phase)
    stores = [
        pltpu.make_async_copy(gg, gg_hbm.at[0], out_sem.at[0]),
        pltpu.make_async_copy(gu, gu_hbm.at[0], out_sem.at[1]),
        pltpu.make_async_copy(gd, gd_hbm.at[0], out_sem.at[2]),
    ]
    for store in stores:
        store.start()

    many_m().wait_recv()
    for b in range(4):
        source = (b % 2) * 2 + b // 2
        total = mrecv[source].astype(F32)
        for gg_ in range(1, 4):
            total += mrecv[gg_ * 4 + source].astype(F32)
        mixed_ref[:, b * QUART : (b + 1) * QUART] = total.astype(BF16)
    many_r().wait_recv()
    route_total = jnp.sum(rrecv[...], axis=0)
    mine = jnp.zeros((TOP, BLK), F32)
    for b in range(4):
        mine = jnp.where(ex % 4 == b, route_total[:TOP, b * BLK : (b + 1) * BLK], mine)
    grw_ref[...] = mine
    for p in range(PH):
        many_z(p).wait_recv()
        for h in range(2):
            total = drecv[p, 5 * h].astype(F32)
            for i in range(1, 5):
                total += drecv[p, 5 * h + i].astype(F32)
            start = h * HALF + p * PCOL
            dx_ref[:, start : start + PCOL] = total.astype(BF16)

    many_gz().wait_send()
    many_w(1, 15).wait_send()
    many_g(1, 15).wait_send()
    cp_all = remote(xr.at[0], xr.at[1], sxf.at[0], rxf.at[0], partner)
    cp_all.wait_send()
    cp_all = remote(gr.at[0], gr.at[1], sgf.at[0], rgf.at[0], partner)
    cp_all.wait_send()
    many_yp(0, 4).wait_send()
    many_yz(0, 4).wait_send()
    many_y(1, 15).wait_send()
    many_dp(0, 4 * PH).wait_send()
    many_v(1, 15).wait_send()
    many_m().wait_send()
    many_r().wait_send()
    for p in range(PH):
        many_d(p, 1, 15).wait_send()
        many_pre(p).wait_send()
        many_z(p).wait_send()
    for store in stores:
        store.wait()


def hand_over(*refs):
    count = (len(refs) - 2) // 3
    held, (read, write) = refs[2 * count : 3 * count], refs[3 * count :]
    ins = [pltpu.make_async_copy(refs[i], held[i], read.at[i]) for i in range(count)]
    outs = [pltpu.make_async_copy(held[i], refs[count + i], write.at[i]) for i in range(count)]
    for copy in ins:
        copy.start()
    for i in range(count):
        ins[i].wait()
        outs[i].start()
    for copy in outs:
        copy.wait()


def body(tokens, routes, route_weight, w_gate, w_up, w_down, grad_out):
    any_ = pl.BlockSpec(memory_space=pl.ANY)
    vmem = pl.BlockSpec(memory_space=pltpu.VMEM)
    chunk = (NDP, T8, 8, HALF)
    quart = (NDP, T8, 8, QUART)
    phased = (PH * NDP, T8, 8, PCOL)
    dma = pltpu.SemaphoreType.DMA
    V = pltpu.VMEM
    results = pl.pallas_call(
        kernel,
        out_shape=(
            jax.ShapeDtypeStruct((BLK, D), BF16),
            jax.ShapeDtypeStruct((BLK, D), BF16),
            jax.ShapeDtypeStruct((TOP, BLK), F32),
            jax.ShapeDtypeStruct((1, FF, D), BF16),
            jax.ShapeDtypeStruct((1, FF, D), BF16),
            jax.ShapeDtypeStruct((1, FF, D), BF16),
        ),
        in_specs=[any_, vmem, vmem, any_, any_, any_, any_],
        out_specs=(vmem, vmem, vmem, any_, any_, any_),
        scratch_shapes=[
            V((TOK, HALF), BF16), V((2, BLK, HALF), BF16), V((NEX, BLK, HALF), BF16),
            V((FF, D), BF16), V((FF, D), BF16), V((FF, D), BF16),
            V((NDP, TOK), F32), V((NDP, TOK), F32), V((NDP, TOK), F32), V((NDP, T8, 8, TOK), BF16), V((4, TOK, ROWS), BF16),
            V(chunk, BF16), V((2,) + chunk, BF16), V(chunk, BF16), V((2,) + chunk, BF16),
            V((NDP, 8, 128), F32), V((NDP, 8, 128), F32), V((NDP, 8, 128), F32), V((NDP, 8, 128), F32),
            V(chunk, BF16), V(chunk, BF16), V(quart, BF16), V(quart, BF16), V(quart, BF16), V(quart, BF16),
            V(phased, BF16), V(phased, BF16), V(phased, BF16), V(phased, BF16),
            V((4, ROWS, FF), F32), V((4, ROWS, FF), F32),
            V((4, FF, ROWS), BF16), V((4, FF, ROWS), BF16), V((4, FF, ROWS), BF16), V((4, ROWS, FF), BF16), V((4, ROWS, FF), BF16),
            V((NEX, BLK, QUART), BF16), V((NEX, BLK, QUART), BF16), V((PH, NEX, BLK, PCOL), BF16), V((PH, 3, 2, BLK, PCOL), BF16), V((PH, 10, BLK, PCOL), BF16),
            V((4, 8, 128), F32), V((NEX, 8, 128), F32),
            V((FF, D), BF16), V((FF, D), BF16), V((FF, D), BF16),
            dma((6,)), dma((3,)),
            dma((1,)), dma((1,)), dma((4,)), dma((4,)), dma((1,)), dma((4,)),
            dma((1,)), dma((4,)), dma((1,)), dma((4,)), dma((1,)), dma((4,)),
            dma((1,)), dma((4,)), dma((1,)), dma((4,)), dma((1,)), dma((1,)), dma((1,)), dma((4 * PH,)),
            dma((PH,)), dma((PH,)), dma((1,)), dma((1,)),
            dma((1,)), dma((1,)), dma((PH,)), dma((PH,)), dma((PH,)), dma((PH,)), dma((1,)), dma((1,)),
        ],
        compiler_params=pltpu.CompilerParams(
            collective_id=0, has_side_effects=True, vmem_limit_bytes=63_000_000
        ),
    )(tokens, routes.T, route_weight.T, w_gate, w_up, w_down, grad_out)
    mixed, dx, grw, gg, gu, gd = pl.pallas_call(
        hand_over,
        out_shape=tuple(jax.ShapeDtypeStruct(r.shape, r.dtype) for r in results),
        in_specs=[any_] * 6,
        out_specs=(any_,) * 6,
        scratch_shapes=[V(r.shape, r.dtype) for r in results] + [dma((6,)), dma((6,))],
    )(*results)
    return mixed, dx, grw.T, gg, gu, gd


def solution(mesh):
    rows = P(("dp", "expert"), None)
    block = P(("dp", "expert"), None, None)
    return jax.shard_map(
        body,
        mesh=mesh,
        in_specs=(P("dp", None), P("dp", None), P("dp", None), block, block, block, rows),
        out_specs=(rows, rows, rows, block, block, block),
        check_vma=False,
    )
```

```python
import jax
import jax.numpy as jnp
from jax import lax
from jax.experimental import pallas as pl
from jax.experimental.pallas import tpu as pltpu
from jax.sharding import PartitionSpec as P

MESH = pl.DeviceIdType.MESH
F32 = jnp.float32
BF16 = jnp.bfloat16

TOK = 512
D = 2048
HALF = 1024
FF = 352
TOP = 6
CAP = 72
T8 = CAP // 8
NDP = 16
NEX = 16
BLK = TOK // NEX
ROWS = 4 * CAP
COLS = 512
QUART = 512
PH = 4
PCOL = HALF // PH


def rows_of(ref_value):
    return ref_value.reshape(-1, ref_value.shape[-1])


def nt(a, b):
    return lax.dot_general(a, b, (((1,), (1,)), ((), ())), preferred_element_type=F32)


def tn(a, b):
    return lax.dot_general(a, b, (((0,), (0,)), ((), ())), preferred_element_type=F32)


def nn(a, b):
    return jnp.dot(a, b, preferred_element_type=F32)


def kernel(
    tok_hbm, routes_ref, weight_ref, wg_hbm, wu_hbm, wd_hbm, g_hbm,
    mixed_ref, dx_ref, grw_ref, gg_hbm, gu_hbm, gd_hbm,
    tok, gloc, gall, wg, wu, wd, hits, rank, wtok, sel, selt,
    xs, xr, gs, gr, ws, wr, vs, vret,
    yo, ypi, yzo, yzi, yq, yret, do, dpo, dpi, dret,
    gate_s, up_s, hwt, dgt, dut, dgs, dus,
    mst, mrecv, dst_, pre, drecv, rst, rrecv, gg, gu, gd,
    in_sem, out_sem, sgz, rgz, sx, rx, sxf, rxf, sw, rw, sg, rg, sgf, rgf,
    syp, ryp, syz, ryz, sy, ry, sdp, rdp, sd, rd, sv, rv, sm, rm, spre, rpre, sz, rz, sr, rr,
):
    dp = lax.axis_index("dp")
    ex = lax.axis_index("expert")
    px, py = dp % 4, dp // 4
    core = ex % 2
    other = 1 - core
    group = ex // 4
    partner = (dp, ex + 1 - 2 * core)
    ez = ex // 2
    odd = ez % 2
    across = (dp, ex + 2 - 4 * odd)

    def gray(v):
        return v + (v // 2) * (1 - 2 * (v % 2))

    def to_dp(k):
        return ((py + gray(k // 4)) % 4) * 4 + (px + gray(k % 4)) % 4

    def from_dp(k):
        return ((py + 4 - gray(k // 4)) % 4) * 4 + (px + 4 - gray(k % 4)) % 4

    def to_ex(m):
        return (ex + m) % NEX

    def remote(src, dst, ssem, rsem, where):
        return pltpu.make_async_remote_copy(
            src_ref=src, dst_ref=dst, send_sem=ssem, recv_sem=rsem,
            device_id=where, device_id_type=MESH,
        )

    def cp_gz(m):
        e2 = to_ex(m)
        return remote(gloc.at[e2 % 2], gall.at[ex], sgz.at[0], rgz.at[0], (dp, e2))

    def many_gz():
        return remote(gall.at[pl.ds(0, 15)], gall.at[pl.ds(0, 15)], sgz.at[0], rgz.at[0], partner)

    def many_x(k, n):
        at = pl.ds(k, n)
        return remote(xs.at[at], xr.at[core, at], sx.at[k // 4], rx.at[k // 4], (to_dp(k), ex))

    def cp_xf(q):
        half = xr.at[core, pl.ds(q * 4, 4)]
        return remote(half, half, sxf.at[0], rxf.at[q], partner)

    def many_w(k, n):
        at = pl.ds(k, n)
        return remote(ws.at[at], wr.at[at], sw.at[0], rw.at[k // 4], (to_dp(k), ex))

    def many_g(k, n):
        at = pl.ds(k, n)
        return remote(gs.at[at], gr.at[core, at], sg.at[0], rg.at[k // 4], (to_dp(k), ex))

    def cp_gf(q):
        half = gr.at[core, pl.ds(q * 4, 4)]
        return remote(half, half, sgf.at[0], rgf.at[q], partner)

    def many_yp(q, n):
        at = pl.ds(q * 4, 4 * n)
        return remote(xs.at[at], ypi.at[at], syp.at[0], ryp.at[q], partner)

    def many_yz(q, n):
        at = pl.ds(q * 4, 4 * n)
        return remote(yzo.at[at], yzi.at[at], syz.at[0], ryz.at[q], across)

    def many_y(k, n):
        at = pl.ds(k, n)
        return remote(yq.at[at], yret.at[at], sy.at[0], ry.at[0], (from_dp(k), ex))

    def many_dp(i, n):
        at = pl.ds(i * 4, 4 * n)
        return remote(dpo.at[at], dpi.at[at], sdp.at[0], rdp.at[i], partner)

    def many_d(p, k, n):
        at = pl.ds(p * NDP + k, n)
        return remote(do.at[at], dret.at[at], sd.at[p], rd.at[p], (from_dp(k), ex))

    def many_v(k, n):
        at = pl.ds(k, n)
        return remote(vs.at[at], vret.at[at], sv.at[0], rv.at[0], (from_dp(k), ex))

    def cp_m(m):
        e2 = to_ex(m)
        return remote(mst.at[e2], mrecv.at[ex], sm.at[0], rm.at[0], (dp, e2))

    def many_m():
        return remote(mst.at[pl.ds(0, 15)], mrecv.at[pl.ds(0, 15)], sm.at[0], rm.at[0], partner)

    def chip(n, z, c):
        return (z + (1 - 2 * c) * n + 8) % 8

    def cp_pre(p, i, d, to):
        src = dst_.at[p, pl.ds(2 * chip(d, ez, core), 2)]
        return remote(src, pre.at[p, i], spre.at[p], rpre.at[p], (dp, 2 * chip(to, ez, core) + core))

    def many_pre(p):
        return remote(pre.at[p], pre.at[p], spre.at[p], rpre.at[p], partner)

    def cp_z(p, i, d, c2):
        e2 = 2 * chip(d, ez, core) + c2
        return remote(dst_.at[p, e2], drecv.at[p, core * 5 + i], sz.at[p], rz.at[p], (dp, e2))

    def many_z(p):
        at = pl.ds(0, 9)
        return remote(drecv.at[p, at], drecv.at[p, at], sz.at[p], rz.at[p], partner)

    def cp_r(m):
        e2 = to_ex(m)
        return remote(rst.at[e2 // 4], rrecv.at[ex], sr.at[0], rr.at[0], (dp, e2))

    def many_r():
        at = pl.ds(0, 15)
        return remote(rrecv.at[at], rrecv.at[at], sr.at[0], rr.at[0], partner)

    def by_group(q, fn):
        @pl.when(q == 0)
        def _():
            fn(1, 3)

        @pl.when(q > 0)
        def _():
            fn(q * 4, 4)

    def loop(lo, hi, fn):
        def step(i, carry):
            fn(i)
            return carry

        lax.fori_loop(lo, hi, step, 0)

    loads = [
        pltpu.make_async_copy(g_hbm.at[:, pl.ds(0, HALF)], gloc.at[0], in_sem.at[0]),
        pltpu.make_async_copy(g_hbm.at[:, pl.ds(HALF, HALF)], gloc.at[1], in_sem.at[1]),
        pltpu.make_async_copy(tok_hbm.at[:, pl.ds(pl.multiple_of(core * HALF, HALF), HALF)], tok, in_sem.at[2]),
        pltpu.make_async_copy(wg_hbm.at[0], wg, in_sem.at[3]),
        pltpu.make_async_copy(wu_hbm.at[0], wu, in_sem.at[4]),
        pltpu.make_async_copy(wd_hbm.at[0], wd, in_sem.at[5]),
    ]
    for load in loads:
        load.start()

    barrier = pltpu.get_barrier_semaphore()

    def greet(k):
        pl.semaphore_signal(barrier, inc=1, device_id=(to_dp(k), ex), device_id_type=MESH)
        pl.semaphore_signal(barrier, inc=1, device_id=(dp, to_ex(k)), device_id_type=MESH)

    loop(1, NDP, greet)

    def find(k):
        named = routes_ref[...] == to_dp(k) * 4 + group
        hits[pl.ds(k, 1), :] = jnp.sum(named.astype(F32), axis=0, keepdims=True)
        wtok[pl.ds(k, 1), :] = jnp.sum(jnp.where(named, weight_ref[...], 0.0), axis=0, keepdims=True)

    loop(0, NDP, find)
    before = lax.broadcasted_iota(jnp.int32, (TOK, TOK), 0) < lax.broadcasted_iota(jnp.int32, (TOK, TOK), 1)
    ranks = nn(hits[...].astype(BF16), before.astype(F32).astype(BF16))
    rank[...] = jnp.where(hits[...] > 0.5, ranks, -1.0)

    loads[0].wait()
    loads[1].wait()
    pl.semaphore_wait(barrier, 2 * (NDP - 1))
    loop(1, NEX, lambda m: cp_gz(m).start())
    gall[pl.ds(ex, 1)] = gloc[pl.ds(core, 1)]
    loads[2].wait()

    eye = (
        lax.broadcasted_iota(jnp.int32, (CAP, 128), 0) == lax.broadcasted_iota(jnp.int32, (CAP, 128), 1)
    ).astype(F32)

    def to_row(col):
        return jnp.broadcast_to(jnp.sum(eye * col, axis=0, keepdims=True), (8, 128))

    def to_col(row):
        return jnp.sum(eye * row, axis=1, keepdims=True)

    slot = lax.broadcasted_iota(jnp.int32, (CAP, TOK), 0).astype(F32)

    def send_x(q):
        at = pl.ds(q * 4, 4)
        hot = []
        for r in range(4):
            k = q * 4 + r
            one = (slot == rank[pl.ds(k, 1), :]).astype(F32)
            w = jnp.sum(one * wtok[pl.ds(k, 1), :], axis=1, keepdims=True)
            ws[pl.ds(k, 1)] = to_row(w)[None]
            hot.append(one)
        s = jnp.concatenate(hot, axis=0).astype(BF16)
        sel[at] = s.reshape(4, T8, 8, TOK)
        xs[at] = nn(s, tok[...]).astype(BF16).reshape(4, T8, 8, HALF)

        def go(k):
            many_x(k, 1).start()
            many_w(k, 1).start()

        loop(jnp.maximum(q * 4, 1), q * 4 + 4, go)
        selt[q] = s.T

    loop(0, 4, lambda q: send_x(q + core * (3 - 2 * q)))
    xr[pl.ds(core, 1), 0:1] = xs[0:1][None]
    wr[0:1] = ws[0:1]

    many_gz().wait_recv()

    def send_g(q):
        at = pl.ds(q * 4, 4)
        gs[at] = nn(rows_of(sel[at]), rows_of(gall[...])).astype(BF16).reshape(4, T8, 8, HALF)
        lo, hi = jnp.maximum(q * 4, 1), q * 4 + 4
        loop(lo, hi, lambda k: many_g(k + core * (lo + hi - 1 - 2 * k), 1).start())

    def pass_x(q):
        by_group(q, lambda k, n: many_x(k, n).wait_recv())
        by_group(q, lambda k, n: many_w(k, n).wait_recv())
        cp_xf(q).start()

    loop(0, 4, lambda q: send_g(q + core * (3 - 2 * q)))
    gr[pl.ds(core, 1), 0:1] = gs[0:1][None]
    for load in loads[3:]:
        load.wait()

    def weight_col(q):
        return jnp.concatenate([to_col(wr[pl.ds(q * 4 + r, 1)][0, 0:1]) for r in range(4)], axis=0)

    def forward(q):
        cp_xf(q).wait_recv()
        at = pl.ds(q * 4, 4)
        x0 = rows_of(xr[0, at])
        x1 = rows_of(xr[1, at])
        gate = nt(x0, wg[:, :HALF]) + nt(x1, wg[:, HALF:])
        up = nt(x0, wu[:, :HALF]) + nt(x1, wu[:, HALF:])
        gate_s[q] = gate
        up_s[q] = up
        hidden = gate * jax.nn.sigmoid(gate) * up
        hw = (weight_col(q) * hidden).astype(BF16)
        hwt[q] = hw.T
        send = pl.multiple_of(other * HALF, HALF)
        keep = pl.multiple_of(core * HALF, HALF)
        by_group(q, lambda k, n: many_x(k, n).wait_send())
        xs[at] = nn(hw, wd[:, pl.ds(send, HALF)]).astype(BF16).reshape(4, T8, 8, HALF)
        many_yp(q, 1).start()
        yo[at] = nn(hw, wd[:, pl.ds(keep, HALF)]).astype(BF16).reshape(4, T8, 8, HALF)

    def cross_y(q):
        many_yp(q, 1).wait_recv()
        at = pl.ds(q * 4, 4)
        send = pl.ds(pl.multiple_of((1 - odd) * QUART, QUART), QUART)
        keep = pl.ds(pl.multiple_of(odd * QUART, QUART), QUART)
        yzo[at] = (yo[at, :, :, send].astype(F32) + ypi[at, :, :, send].astype(F32)).astype(BF16)
        many_yz(q, 1).start()
        yq[at] = (yo[at, :, :, keep].astype(F32) + ypi[at, :, :, keep].astype(F32)).astype(BF16)

    def return_y(q):
        many_yz(q, 1).wait_recv()
        at = pl.ds(q * 4, 4)
        yq[at] = (yq[at].astype(F32) + yzi[at].astype(F32)).astype(BF16)
        loop(jnp.maximum(q * 4, 1), q * 4 + 4, lambda k: many_y(k, 1).start())

    def forward_step(q):
        @pl.when(q < 4)
        def _():
            pass_x(q)

        @pl.when((q >= 1) & (q < 5))
        def _():
            forward(q - 1)

        @pl.when((q >= 2) & (q < 6))
        def _():
            cross_y(q - 2)

        @pl.when(q >= 3)
        def _():
            return_y(q - 3)

    loop(0, 7, forward_step)
    yret[0:1] = yq[0:1]

    def pass_g(q):
        by_group(q, lambda k, n: many_g(k, n).wait_recv())
        cp_gf(q).start()

    def backward(q):
        cp_gf(q).wait_recv()
        at = pl.ds(q * 4, 4)
        dh = nt(rows_of(gr[0, at]), wd[:, :HALF]) + nt(rows_of(gr[1, at]), wd[:, HALF:])
        gate = gate_s[q]
        up = up_s[q]
        sigma = jax.nn.sigmoid(gate)
        silu = gate * sigma
        slope = sigma * (1.0 + gate * (1.0 - sigma))
        dot = jnp.sum(silu * up * dh, axis=1, keepdims=True)
        for r in range(4):
            vs[pl.ds(q * 4 + r, 1)] = to_row(dot[r * CAP : (r + 1) * CAP])[None]
        loop(jnp.maximum(q * 4, 1), q * 4 + 4, lambda k: many_v(k, 1).start())
        dh = weight_col(q) * dh
        dg = (dh * up * slope).astype(BF16)
        du = (dh * silu).astype(BF16)
        dgt[q] = dg.T
        dut[q] = du.T
        dgs[q] = dg
        dus[q] = du

    def backward_step(q):
        @pl.when(q < 4)
        def _():
            pass_g(q)

        @pl.when(q >= 1)
        def _():
            backward(q - 1)

    loop(0, 5, backward_step)

    def input_grad(i):
        p, q = i // 4, i % 4
        at = pl.ds(i * 4, 4)
        send = pl.ds(pl.multiple_of(other * HALF + p * PCOL, PCOL), PCOL)
        keep = pl.ds(pl.multiple_of(core * HALF + p * PCOL, PCOL), PCOL)
        dpo[at] = (nn(dgs[q], wg[:, send]) + nn(dus[q], wu[:, send])).astype(BF16).reshape(4, T8, 8, PCOL)
        many_dp(i, 1).start()
        do[at] = (nn(dgs[q], wg[:, keep]) + nn(dus[q], wu[:, keep])).astype(BF16).reshape(4, T8, 8, PCOL)

    def return_d(i):
        p, q = i // 4, i % 4
        many_dp(i, 1).wait_recv()
        at = pl.ds(i * 4, 4)
        do[at] = (do[at].astype(F32) + dpi[at].astype(F32)).astype(BF16)

        @pl.when(p < 1)
        def _():
            loop(jnp.maximum(q * 4, 1), q * 4 + 4, lambda k: many_d(p, k, 1).start())

    def input_step(i):
        @pl.when(i < 4 * PH)
        def _():
            input_grad(i)

        @pl.when(i >= 1)
        def _():
            return_d(i - 1)

    loop(0, 4 * PH + 1, input_step)
    for p in range(PH):
        dret[p * NDP : p * NDP + 1] = do[p * NDP : p * NDP + 1]
    vret[0:1] = vs[0:1]

    def combine(back, base):
        total = nn(selt[0], rows_of(back[pl.ds(base, 4)]))
        for q in range(1, 4):
            total += nn(selt[q], rows_of(back[pl.ds(base + q * 4, 4)]))
        return total.astype(BF16).reshape(NEX, BLK, back.shape[-1])

    def go_d(p):
        loop(1, NDP, lambda k: many_d(p, k + core * (NDP - 2 * k), 1).start())

    many_y(1, 15).wait_recv()
    go_d(1)
    mst[...] = combine(yret, 0)
    loop(1, NEX, lambda m: cp_m(m).start())
    mrecv[pl.ds(ex, 1)] = mst[pl.ds(ex, 1)]

    rst[...] = jnp.zeros_like(rst)
    many_v(1, 15).wait_recv()

    def route_grad(k):
        col = to_col(vret[pl.ds(k, 1)][0, 0:1])
        row = jnp.sum(rows_of(sel[pl.ds(k, 1)]).astype(F32) * col, axis=0, keepdims=True)
        add = jnp.where(routes_ref[...] == to_dp(k) * 4 + group, row, 0.0)
        for b in range(4):
            rst[b, :TOP] += add[:, b * 128 : (b + 1) * 128]

    loop(0, NDP, route_grad)
    loop(1, NEX, lambda m: cp_r(m).start())
    rrecv[pl.ds(ex, 1)] = rst[pl.ds(group, 1)]

    def grads(n):
        h = n // (HALF // COLS)
        cols = pl.ds(pl.multiple_of((n % (HALF // COLS)) * COLS, COLS), COLS)
        outs = pl.ds(pl.multiple_of(n * COLS, COLS), COLS)

        def total(left, right):
            acc = nn(left[0], rows_of(right[h, 0:4, :, :, cols]))
            for q in range(1, 4):
                acc += nn(left[q], rows_of(right[h, q * 4 : q * 4 + 4, :, :, cols]))
            return acc.astype(BF16)

        gd[:, outs] = total(hwt, gr)
        gg[:, outs] = total(dgt, xr)
        gu[:, outs] = total(dut, xr)

    def arrive(p):
        many_d(p, 1, 15).wait_recv()

        @pl.when(p + 2 < PH)
        def _():
            go_d(p + 2)

        dst_[pl.ds(p, 1)] = combine(dret, p * NDP)[None]
        cp_pre(p, 0, -4, -1).start()
        cp_pre(p, 1, -2, -1).start()
        cp_pre(p, 2, 3, 1).start()
        cp_z(p, 3, 1, 0).start()
        cp_z(p, 3, 1, 1).start()
        cp_z(p, 4, 0, other).start()
        drecv[pl.ds(p, 1), pl.ds(core * 5 + 4, 1)] = dst_[pl.ds(p, 1), pl.ds(ex, 1)]
        grads(p)

    def pass_on(p):
        many_pre(p).wait_recv()
        for i, d in ((0, -3), (1, -1), (2, 2)):
            at = pl.ds(2 * chip(d, ez, core), 2)
            joined = dst_[pl.ds(p, 1), at].astype(F32) + pre[pl.ds(p, 1), i].astype(F32)
            dst_[pl.ds(p, 1), at] = joined.astype(BF16)
            cp_z(p, i, d, 0).start()
            cp_z(p, i, d, 1).start()

    def phase(p):
        @pl.when(p < PH)
        def _():
            arrive(p)

        @pl.when(p >= 1)
        def _():
            pass_on(p - 1)

    loop(0, PH + 1, phase)
    stores = [
        pltpu.make_async_copy(gg, gg_hbm.at[0], out_sem.at[0]),
        pltpu.make_async_copy(gu, gu_hbm.at[0], out_sem.at[1]),
        pltpu.make_async_copy(gd, gd_hbm.at[0], out_sem.at[2]),
    ]
    for store in stores:
        store.start()

    many_m().wait_recv()
    for b in range(4):
        source = (b % 2) * 2 + b // 2
        total = mrecv[source].astype(F32)
        for gg_ in range(1, 4):
            total += mrecv[gg_ * 4 + source].astype(F32)
        mixed_ref[:, b * QUART : (b + 1) * QUART] = total.astype(BF16)
    many_r().wait_recv()
    route_total = jnp.sum(rrecv[...], axis=0)
    mine = jnp.zeros((TOP, BLK), F32)
    for b in range(4):
        mine = jnp.where(ex % 4 == b, route_total[:TOP, b * BLK : (b + 1) * BLK], mine)
    grw_ref[...] = mine
    for p in range(PH):
        many_z(p).wait_recv()
        for h in range(2):
            total = drecv[p, 5 * h].astype(F32)
            for i in range(1, 5):
                total += drecv[p, 5 * h + i].astype(F32)
            start = h * HALF + p * PCOL
            dx_ref[:, start : start + PCOL] = total.astype(BF16)

    many_gz().wait_send()
    many_w(1, 15).wait_send()
    many_g(1, 15).wait_send()
    cp_all = remote(xr.at[0], xr.at[1], sxf.at[0], rxf.at[0], partner)
    cp_all.wait_send()
    cp_all = remote(gr.at[0], gr.at[1], sgf.at[0], rgf.at[0], partner)
    cp_all.wait_send()
    many_yp(0, 4).wait_send()
    many_yz(0, 4).wait_send()
    many_y(1, 15).wait_send()
    many_dp(0, 4 * PH).wait_send()
    many_v(1, 15).wait_send()
    many_m().wait_send()
    many_r().wait_send()
    for p in range(PH):
        many_d(p, 1, 15).wait_send()
        many_pre(p).wait_send()
        many_z(p).wait_send()
    for store in stores:
        store.wait()


def hand_over(*refs):
    count = (len(refs) - 2) // 3
    held, (read, write) = refs[2 * count : 3 * count], refs[3 * count :]
    ins = [pltpu.make_async_copy(refs[i], held[i], read.at[i]) for i in range(count)]
    outs = [pltpu.make_async_copy(held[i], refs[count + i], write.at[i]) for i in range(count)]
    for copy in ins:
        copy.start()
    for i in range(count):
        ins[i].wait()
        outs[i].start()
    for copy in outs:
        copy.wait()


def body(tokens, routes, route_weight, w_gate, w_up, w_down, grad_out):
    any_ = pl.BlockSpec(memory_space=pl.ANY)
    vmem = pl.BlockSpec(memory_space=pltpu.VMEM)
    chunk = (NDP, T8, 8, HALF)
    quart = (NDP, T8, 8, QUART)
    phased = (PH * NDP, T8, 8, PCOL)
    dma = pltpu.SemaphoreType.DMA
    V = pltpu.VMEM
    results = pl.pallas_call(
        kernel,
        out_shape=(
            jax.ShapeDtypeStruct((BLK, D), BF16),
            jax.ShapeDtypeStruct((BLK, D), BF16),
            jax.ShapeDtypeStruct((TOP, BLK), F32),
            jax.ShapeDtypeStruct((1, FF, D), BF16),
            jax.ShapeDtypeStruct((1, FF, D), BF16),
            jax.ShapeDtypeStruct((1, FF, D), BF16),
        ),
        in_specs=[any_, vmem, vmem, any_, any_, any_, any_],
        out_specs=(vmem, vmem, vmem, any_, any_, any_),
        scratch_shapes=[
            V((TOK, HALF), BF16), V((2, BLK, HALF), BF16), V((NEX, BLK, HALF), BF16),
            V((FF, D), BF16), V((FF, D), BF16), V((FF, D), BF16),
            V((NDP, TOK), F32), V((NDP, TOK), F32), V((NDP, TOK), F32), V((NDP, T8, 8, TOK), BF16), V((4, TOK, ROWS), BF16),
            V(chunk, BF16), V((2,) + chunk, BF16), V(chunk, BF16), V((2,) + chunk, BF16),
            V((NDP, 8, 128), F32), V((NDP, 8, 128), F32), V((NDP, 8, 128), F32), V((NDP, 8, 128), F32),
            V(chunk, BF16), V(chunk, BF16), V(quart, BF16), V(quart, BF16), V(quart, BF16), V(quart, BF16),
            V(phased, BF16), V(phased, BF16), V(phased, BF16), V(phased, BF16),
            V((4, ROWS, FF), F32), V((4, ROWS, FF), F32),
            V((4, FF, ROWS), BF16), V((4, FF, ROWS), BF16), V((4, FF, ROWS), BF16), V((4, ROWS, FF), BF16), V((4, ROWS, FF), BF16),
            V((NEX, BLK, QUART), BF16), V((NEX, BLK, QUART), BF16), V((PH, NEX, BLK, PCOL), BF16), V((PH, 3, 2, BLK, PCOL), BF16), V((PH, 10, BLK, PCOL), BF16),
            V((4, 8, 128), F32), V((NEX, 8, 128), F32),
            V((FF, D), BF16), V((FF, D), BF16), V((FF, D), BF16),
            dma((6,)), dma((3,)),
            dma((1,)), dma((1,)), dma((4,)), dma((4,)), dma((1,)), dma((4,)),
            dma((1,)), dma((4,)), dma((1,)), dma((4,)), dma((1,)), dma((4,)),
            dma((1,)), dma((4,)), dma((1,)), dma((4,)), dma((1,)), dma((1,)), dma((1,)), dma((4 * PH,)),
            dma((PH,)), dma((PH,)), dma((1,)), dma((1,)),
            dma((1,)), dma((1,)), dma((PH,)), dma((PH,)), dma((PH,)), dma((PH,)), dma((1,)), dma((1,)),
        ],
        compiler_params=pltpu.CompilerParams(
            collective_id=0, has_side_effects=True, vmem_limit_bytes=63_000_000
        ),
    )(tokens, routes.T, route_weight.T, w_gate, w_up, w_down, grad_out)
    mixed, dx, grw, gg, gu, gd = pl.pallas_call(
        hand_over,
        out_shape=tuple(jax.ShapeDtypeStruct(r.shape, r.dtype) for r in results),
        in_specs=[any_] * 6,
        out_specs=(any_,) * 6,
        scratch_shapes=[V(r.shape, r.dtype) for r in results] + [dma((6,)), dma((6,))],
    )(*results)
    return mixed, dx, grw.T, gg, gu, gd


def solution(mesh):
    rows = P(("dp", "expert"), None)
    block = P(("dp", "expert"), None, None)
    return jax.shard_map(
        body,
        mesh=mesh,
        in_specs=(P("dp", None), P("dp", None), P("dp", None), block, block, block, rows),
        out_specs=(rows, rows, rows, block, block, block),
        check_vma=False,
    )
```
